512 devices in a mesh: group: 32 (over y, x, core), tp: 16 (over z).
Axes of the slice: x: 4, y: 4, z: 16, core: 2. Of those that a mesh axis runs over, the one named last changes fastest.
Arguments:
- lengths: int32 [416], P('group'), may hold values from 1 to 510, as said below
- destination: int32 [416], replicated, may hold values from 0 to 415, as said below
- page_before: int32 [416, 4], P('group'), may hold values from 0 to 15, as said below
- page_after: int32 [416, 4], P('group'), may hold values from 0 to 15, as said below
- kv_cache: bfloat16 [32, 16, 16, 128, 256], P('group', 'tp'), may hold values from -8 to 8, as said below
- queries: bfloat16 [2, 416, 4096], P(None, 'group', 'tp'), may hold values from -32 to 32
- new_kv: bfloat16 [2, 416, 8, 256], P(None, 'group'), may hold values from -8 to 8, as said below
- residual: bfloat16 [2, 416, 5120], P(None, 'group'), may hold values from -16 to 16
- out_weight: bfloat16 [4096, 5120], P('tp'), may hold values from -0.5 to 0.5
- norm_gain: bfloat16 [5120], P('tp'), may hold values from 0.099609375 to 1.8984375
Outputs:
- kv_after: bfloat16 [32, 16, 16, 128, 256], P('group', 'tp')
- updated: bfloat16 [2, 416, 5120], P(None, 'group', 'tp')
- normed: bfloat16 [2, 416, 5120], P(None, 'group', 'tp')
The draws below stay inside these ranges and needn't reach their ends.
Inputs may be any that keep to these rules, and one draw needn't show every extreme that they name: `lengths`: each row has ceil((length + 2) / 128) pages. `destination`: a permutation of the 416 positions; in each group exactly 11 rows go to other groups, no two of them to the same group, each of these rows has exactly 1 page, and the other rows stay in their group. `page_before`: for each group, the entries j below the page counts of its 13 rows (before the move) name each of its 16 slots once; other entries are not read. `page_after`: for each group, the entries j below the page counts of its 13 rows (after the move) name each of its 16 slots once; other entries are not read. `kv_cache`: entry [g, t] holds KV head t // 2 of group g, keys in the first 128 entries of a token and values in the last; entries t = 2k and 2k + 1 are equal. `new_kv`: keys then values of each KV head.
All inputs are finite; a program needn't handle non-finite values.
Results may differ from the reference program's by a relative error of at most 0.005.
Values may be sent and summed in bfloat16 or wider, within the bound.
A program may use at most 64 MiB of HBM per device.

```python
import math
import jax
import jax.numpy as jnp
from jax import lax

D = 5120
HD = 128
QH_DEV = 2
QH = 32
KVH = 8
PAGE = 128
STEPS = 2
ROWS_GRP = 13
MOVE = 11
PMOVE = 1
SLOTS = 16
MAXPAGES = 4
ROWS = 416
N_GROUP = 32
N_TP = 16


def page_table(table_key, row_pages):
    group_count = ROWS // ROWS_GRP
    perm_key, filler_key = jax.random.split(table_key)
    slot_ids = jnp.arange(SLOTS, dtype=jnp.int32)
    perm_scores = jax.random.randint(perm_key, (group_count, SLOTS), 0, 1 << 20) * SLOTS + slot_ids[None, :]
    slot_perm = jnp.argsort(perm_scores, axis=1).astype(jnp.int32)
    grid_pages = row_pages.reshape(group_count, ROWS_GRP)
    starts = jnp.cumsum(grid_pages, axis=1) - grid_pages
    page_ids = jnp.arange(MAXPAGES, dtype=jnp.int32)
    index_grid = jnp.clip(starts[:, :, None] + page_ids[None, None, :], 0, SLOTS - 1)
    picked = jnp.take_along_axis(slot_perm, index_grid.reshape(group_count, ROWS_GRP * MAXPAGES), axis=1)
    picked = picked.reshape(group_count, ROWS_GRP, MAXPAGES)
    filler = jax.random.randint(filler_key, (group_count, ROWS_GRP, MAXPAGES), 0, SLOTS)
    table = jnp.where(page_ids[None, None, :] < grid_pages[:, :, None], picked, filler)
    return table.reshape(ROWS, MAXPAGES).astype(jnp.int32)


def layout_tables(key):
    keys_all = jax.random.split(key, 8)
    group_count = ROWS // ROWS_GRP
    stay_count = ROWS_GRP - MOVE
    spare = SLOTS - MOVE * PMOVE - stay_count
    position_ids = jnp.arange(ROWS_GRP, dtype=jnp.int32)
    order_scores = jax.random.randint(keys_all[0], (group_count, ROWS_GRP), 0, 1 << 20) * ROWS_GRP + position_ids[None, :]
    before_order = jnp.argsort(order_scores, axis=1).astype(jnp.int32)
    after_scores = jax.random.randint(keys_all[1], (group_count, ROWS_GRP), 0, 1 << 20) * ROWS_GRP + position_ids[None, :]
    after_place = jnp.argsort(after_scores, axis=1).astype(jnp.int32)
    relabel = jax.random.permutation(keys_all[2], group_count).astype(jnp.int32)
    rank_of = jnp.argsort(relabel).astype(jnp.int32)
    group_ids = jnp.arange(group_count, dtype=jnp.int32)
    mover_ids = jnp.arange(MOVE, dtype=jnp.int32)
    target_group = relabel[(rank_of[:, None] + mover_ids[None, :] + 1) % group_count]
    mover_dest = target_group * ROWS_GRP + after_place[target_group, mover_ids[None, :]]
    stay_dest = group_ids[:, None] * ROWS_GRP + after_place[:, MOVE:]
    list_dest = jnp.concatenate([mover_dest, stay_dest], axis=1)
    before_index = (group_ids[:, None] * ROWS_GRP + before_order).reshape(-1)
    destination = jnp.zeros((ROWS,), jnp.int32).at[before_index].set(list_dest.reshape(-1))
    forced = jax.random.randint(keys_all[3], (), 0, group_count)
    buckets = jax.random.randint(keys_all[4], (group_count, spare), 0, stay_count)
    stay_pages = 1 + jnp.sum((buckets[:, :, None] == jnp.arange(stay_count, dtype=jnp.int32)[None, None, :]).astype(jnp.int32), axis=1)
    forced_pages = jnp.concatenate([jnp.full((1,), 1 + spare, jnp.int32), jnp.ones((stay_count - 1,), jnp.int32)])
    forced_row = (group_ids == forced)[:, None]
    stay_pages = jnp.where(forced_row, forced_pages[None, :], stay_pages)
    list_pages = jnp.concatenate([jnp.full((group_count, MOVE), PMOVE, jnp.int32), stay_pages], axis=1)
    fill_tokens = jax.random.randint(keys_all[5], (group_count, ROWS_GRP), 1, PAGE - STEPS + 1)
    column = position_ids[None, :]
    fill_tokens = jnp.where(forced_row & (column == MOVE), PAGE - STEPS, fill_tokens)
    fill_tokens = jnp.where(forced_row & (column == MOVE + 1), 1, fill_tokens)
    list_length = (list_pages - 1) * PAGE + fill_tokens
    pages_before = jnp.zeros((ROWS,), jnp.int32).at[before_index].set(list_pages.reshape(-1))
    length_before = jnp.zeros((ROWS,), jnp.int32).at[before_index].set(list_length.reshape(-1).astype(jnp.int32))
    lengths_after = jnp.zeros((ROWS,), jnp.int32).at[destination].set(length_before)
    pages_after = jnp.zeros((ROWS,), jnp.int32).at[destination].set(pages_before)
    table_before = page_table(keys_all[6], pages_before)
    table_after = page_table(keys_all[7], pages_after)
    return (destination, lengths_after, table_before, table_after)


def draw_lengths(key, part):
    shared = layout_tables(key)
    return shared[1]


def draw_destination(key, part):
    shared = layout_tables(key)
    return shared[0]


def draw_page_before(key, part):
    shared = layout_tables(key)
    return shared[2]


def draw_page_after(key, part):
    shared = layout_tables(key)
    return shared[3]


def draw_kv_cache(key, part):
    key = jax.random.fold_in(key, 11)
    array_shape = (ROWS // ROWS_GRP, KVH, SLOTS, PAGE, 2 * HD)
    base_draw = jax.random.normal(key, array_shape, jnp.float32)
    col_scale = jnp.concatenate([jnp.full((HD,), 1.5, jnp.float32), jnp.ones((HD,), jnp.float32)])
    values = jnp.clip(base_draw * col_scale, -8.0, 8.0)
    return jnp.repeat(values, 2, axis=1).astype(jnp.bfloat16)


def draw_queries(key, part):
    key = jax.random.fold_in(key, 12)
    array_shape = (STEPS, ROWS, QH * HD)
    result = jnp.clip(jax.random.normal(key, array_shape, jnp.float32), -6.0, 6.0)
    return result.astype(jnp.bfloat16)


def draw_new_kv(key, part):
    key = jax.random.fold_in(key, 13)
    key_part, value_part = jax.random.split(key)
    array_shape = (STEPS, ROWS, KVH, HD)
    key_rows = jnp.clip(1.5 * jax.random.normal(key_part, array_shape, jnp.float32), -8.0, 8.0)
    value_rows = jnp.clip(jax.random.normal(value_part, array_shape, jnp.float32), -6.0, 6.0)
    return jnp.concatenate([key_rows, value_rows], axis=3).astype(jnp.bfloat16)


def draw_residual(key, part):
    key = jax.random.fold_in(key, 14)
    col_key = jax.random.fold_in(key, 0)
    value_key = jax.random.fold_in(key, 2)
    col_scale = jnp.exp(jax.random.uniform(col_key, (D,), jnp.float32, math.log(0.3), math.log(3.0)))
    base_draw = 0.5 * jax.random.normal(value_key, (STEPS, ROWS, D), jnp.float32)
    return jnp.clip(base_draw * col_scale[None, None, :], -16.0, 16.0).astype(jnp.bfloat16)


def strengthened(drawn, key, source, target, shards_of, factor):
    def block_of(dim):
        return (jnp.arange(drawn.shape[dim]) // (drawn.shape[dim] // shards_of)).reshape((-1,) + (1,) * (drawn.ndim - 1 - dim))

    first = jax.random.permutation(key, shards_of)[block_of(target)]
    far = (block_of(target) + shards_of // 2) % shards_of
    return jnp.where((block_of(source) == first) | (block_of(source) == far), factor * drawn, drawn)


def level_of(rng, extent, cuts, least, top_value):
    gain = 1.0
    for axis_at, blocks in cuts:
        heights = jax.random.uniform(jax.random.fold_in(jax.random.fold_in(rng, 6), axis_at), (blocks,), jnp.float32, least / len(cuts), top_value / len(cuts))
        gain = gain * jnp.repeat(jnp.exp(heights), extent[axis_at] // blocks).reshape((-1,) + (1,) * (len(extent) - 1 - axis_at))
    return gain


def heavy_noise(key, dims, scale, reach, shards, heavy, kind=jnp.bfloat16):
    values = scale * jax.random.normal(key, dims, jnp.float32)
    if shards:
        values = values * level_of(key, dims, shards, -0.22, 0.18)
    return jnp.clip(strengthened(values, jax.random.fold_in(key, 3), *heavy), -reach, reach).astype(kind)


def setup_inputs(seed: int = 0) -> dict:
    key_of = jax.random.split(jax.random.key(seed), 11)
    return {
        "lengths": draw_lengths(jax.random.fold_in(key_of[10], 71), 0),
        "destination": draw_destination(jax.random.fold_in(key_of[10], 71), 0),
        "page_before": draw_page_before(jax.random.fold_in(key_of[10], 71), 0),
        "page_after": draw_page_after(jax.random.fold_in(key_of[10], 71), 0),
        "kv_cache": draw_kv_cache(jax.random.fold_in(key_of[10], 71), 0),
        "queries": draw_queries(jax.random.fold_in(key_of[10], 71), 0),
        "new_kv": draw_new_kv(jax.random.fold_in(key_of[10], 71), 0),
        "residual": draw_residual(jax.random.fold_in(key_of[10], 71), 0),
        "out_weight": heavy_noise(key_of[8], (QH * HD, D), (QH * HD // 16) ** -0.5, 0.5, ((0, 16),), (0, 1, 16, 2.0)),
        "norm_gain": jnp.clip(1.0 + 0.18 * jax.random.normal(key_of[9], (D,), jnp.float32), 0.099609375, 1.8984375).astype(jnp.bfloat16),
    }


def reference(lengths, destination, page_before, page_after, kv_cache, queries, new_kv, residual, out_weight, norm_gain):
    row_ids_all = jnp.arange(ROWS, dtype=jnp.int32)
    anchor = jnp.zeros((ROWS,), jnp.int32).at[destination].set(row_ids_all)
    needed = (lengths + STEPS + PAGE - 1) // PAGE
    page_ids = jnp.arange(MAXPAGES, dtype=jnp.int32)
    page_valid = page_ids[None, :] < needed[:, None]
    source_slot = page_before[anchor]
    source_group = jnp.broadcast_to((anchor // ROWS_GRP)[:, None], source_slot.shape)
    slot_total = N_GROUP * SLOTS
    target = (row_ids_all // ROWS_GRP)[:, None] * SLOTS + page_after
    target = jnp.where(page_valid, target, slot_total).reshape(-1)
    group_of = jnp.zeros((slot_total,), jnp.int32).at[target].set(source_group.reshape(-1), mode='drop')
    slot_of = jnp.zeros((slot_total,), jnp.int32).at[target].set(source_slot.reshape(-1), mode='drop')
    local_rows = jnp.broadcast_to((row_ids_all % ROWS_GRP)[:, None], page_after.shape)
    owner_of = jnp.zeros((slot_total,), jnp.int32).at[target].set(local_rows.reshape(-1), mode='drop')
    number_of = jnp.zeros((slot_total,), jnp.int32).at[target].set(jnp.broadcast_to(page_ids[None, :], page_after.shape).reshape(-1), mode='drop')
    positions = lengths[:, None] + jnp.arange(STEPS, dtype=jnp.int32)[None, :]
    write_slot = jnp.take_along_axis(page_after, positions // PAGE, axis=1)
    fresh_tokens = jnp.transpose(jnp.repeat(new_kv, 2, axis=2), (2, 1, 0, 3))
    copy_of_head = jnp.arange(QH, dtype=jnp.int32) // QH_DEV
    score_scale = HD ** (-0.5)
    step_ids = jnp.arange(STEPS, dtype=jnp.int32)
    group_rows = jnp.arange(ROWS_GRP, dtype=jnp.int32)

    def one_group(group_index):
        slot_start = group_index * SLOTS
        groups_here = lax.dynamic_slice_in_dim(group_of, slot_start, SLOTS)
        slots_here = lax.dynamic_slice_in_dim(slot_of, slot_start, SLOTS)
        group_pages = jnp.transpose(kv_cache[groups_here, :, slots_here], (1, 0, 2, 3))
        rows_start = group_index * ROWS_GRP
        local_lengths = lax.dynamic_slice_in_dim(lengths, rows_start, ROWS_GRP)
        local_write = lax.dynamic_slice_in_dim(write_slot, rows_start, ROWS_GRP, 0)
        local_positions = lax.dynamic_slice_in_dim(positions, rows_start, ROWS_GRP, 0)
        local_fresh = lax.dynamic_slice_in_dim(fresh_tokens, rows_start, ROWS_GRP, 1)
        group_pages = group_pages.at[:, local_write, local_positions % PAGE].set(local_fresh)
        owner_here = lax.dynamic_slice_in_dim(owner_of, slot_start, SLOTS)
        number_here = lax.dynamic_slice_in_dim(number_of, slot_start, SLOTS)
        token_pos = (number_here[:, None] * PAGE + jnp.arange(PAGE, dtype=jnp.int32)[None, :]).reshape(-1)
        token_owner = jnp.repeat(owner_here, PAGE)
        flat_pages = group_pages.reshape(N_TP, SLOTS * PAGE, 2 * HD).astype(jnp.float32)
        cached_keys = flat_pages[:, :, :HD][copy_of_head]
        cached_values = flat_pages[:, :, HD:][copy_of_head]
        query_heads = lax.dynamic_slice_in_dim(queries, rows_start, ROWS_GRP, 1).astype(jnp.float32).reshape(STEPS, ROWS_GRP, QH, HD)
        scores = jnp.einsum('sahd,htd->saht', query_heads, cached_keys) * score_scale
        allowed = (token_owner[None, None, :] == group_rows[None, :, None]) & (token_pos[None, None, :] <= local_lengths[None, :, None] + step_ids[:, None, None])
        scores = jnp.where(allowed[:, :, None, :], scores, -1e+30)
        row_top = lax.optimization_barrier(jnp.max(scores, axis=3, keepdims=True))
        weights = jnp.exp(scores - row_top)
        weight_total = lax.optimization_barrier(jnp.sum(weights, axis=3, keepdims=True))
        probs = weights.astype(jnp.bfloat16).astype(jnp.float32)
        mixed_heads = jnp.einsum('saht,htd->sahd', probs, cached_values) / weight_total
        return (group_pages, mixed_heads.astype(jnp.bfloat16))
    kv_after, mixed_all = lax.map(one_group, jnp.arange(N_GROUP, dtype=jnp.int32))
    attention = jnp.transpose(mixed_all, (1, 0, 2, 3, 4)).reshape(STEPS * ROWS, QH * HD)
    projected = jnp.dot(attention, out_weight, preferred_element_type=jnp.float32)
    hidden = residual.reshape(STEPS * ROWS, D).astype(jnp.float32) + projected
    mean_square = lax.optimization_barrier(jnp.mean(hidden * hidden, axis=1, keepdims=True))
    updated = hidden.astype(jnp.bfloat16).reshape(STEPS, ROWS, D)
    normed = (hidden * lax.rsqrt(mean_square + 1e-06) * norm_gain.astype(jnp.float32)[None, :]).astype(jnp.bfloat16).reshape(STEPS, ROWS, D)
    return (kv_after, updated, normed)
```

```python
import jax
import jax.numpy as jnp
from jax import lax
from jax.experimental import pallas as pl
from jax.experimental.pallas import tpu as pltpu
from jax.sharding import PartitionSpec as P

MESH = pl.DeviceIdType.MESH
NG = 32
NT = 16
ROWS = 13
STEPS = 2
SLOTS = 16
PAGE = 128
HD = 128
RP = 32
D = 5120
COLS = D // NT
BLK = 80
F32 = jnp.float32
BF16 = jnp.bfloat16

SLOT_TO, RET_SRC, B_SRC, B_STAY, OWN, NUM, A_SRC, A_STAY = 0, 32, 64, 80, 96, 112, 128, 144
TABLE = 160


def torus_offsets():
    found = []
    for ky in range(4):
        for kx in range(4):
            for kc in range(2):
                if (ky, kx, kc) != (0, 0, 0):
                    found.append((min(ky, 4 - ky) + min(kx, 4 - kx), ky, kx, kc))
    return sorted(found, key=lambda o: -o[0])


def group_at(g, ky, kx, kc):
    c, x, y = lax.rem(g, 2), lax.rem(g // 2, 4), g // 8
    return lax.rem(y + ky, 4) * 8 + lax.rem(x + kx, 4) * 2 + lax.rem(c + kc, 2)


def group_ahead(g, k):
    return group_at(g, k // 8, lax.rem(k // 2, 4), lax.rem(k, 2))


def group_behind(g, k):
    return group_at(g, 4 - k // 8, 4 - lax.rem(k // 2, 4), lax.rem(k, 2))


def route_kernel(
    lens_in, dest_in, pb_in, q_in, nkv_in, table, pack, mine, fresh,
    lens, dest, pb, q, nkv, anchor, build, sem,
):
    loads = [
        pltpu.make_async_copy(src, dst, sem.at[n])
        for n, (src, dst) in enumerate(
            ((dest_in, dest), (lens_in, lens), (pb_in, pb), (nkv_in, nkv), (q_in, q))
        )
    ]
    for load in loads:
        load.start()
    pack[...] = jnp.zeros_like(pack)
    build[...] = jnp.zeros_like(build)
    for load in loads:
        load.wait()
    g = lax.axis_index("group")
    head = lax.axis_index("tp") // 2
    base = g * ROWS

    def scan(b, carry):
        r = dest[b] - base
        anchor[jnp.where((r >= 0) & (r < ROWS), r, ROWS)] = b
        return carry

    lax.fori_loop(0, NG * ROWS, scan, 0, unroll=16)

    def clear(d, carry):
        table[SLOT_TO + d] = 0
        table[RET_SRC + d] = 0
        return carry

    lax.fori_loop(0, NG, clear, 0, unroll=8)

    def before(i, carry):
        to = dest[base + i]
        r = to - base
        stay = (r >= 0) & (r < ROWS)
        d = to // ROWS
        table[SLOT_TO + d] = pb[0, i]
        table[RET_SRC + d] = i
        table[B_SRC + i] = jnp.where(stay, r, d)
        table[B_STAY + i] = stay.astype(jnp.int32)
        length = lens[jnp.where(stay, r, 0)]
        need = jnp.where(stay, (length + (STEPS + PAGE - 1)) >> 7, 1)
        for j in range(4):
            @pl.when(j < need)
            def _():
                c = pb[j, i]
                table[OWN + c] = i
                table[NUM + c] = j
        return carry

    lax.fori_loop(0, ROWS, before, 0)

    rid = lax.broadcasted_iota(jnp.int32, (RP, 208), 0)
    cid = lax.broadcasted_iota(jnp.int32, (RP, 208), 1)
    pick = (cid == ((rid & 1) * ROWS + (rid >> 1)) * 8 + head) & (rid < STEPS * ROWS)
    tokens = jnp.dot(
        pick.astype(F32).astype(BF16),
        nkv[...].astype(F32).reshape(208, 2 * HD).astype(BF16),
        preferred_element_type=F32,
    )
    fresh[...] = tokens
    for r in range(ROWS):
        anc = anchor[r]
        loc = anc - base
        stay = (loc >= 0) & (loc < ROWS)
        home = anc // ROWS
        table[A_SRC + r] = jnp.where(stay, loc, home)
        table[A_STAY + r] = stay.astype(jnp.int32)
        asked = q[r].astype(F32)
        build[r, 0:2] = asked[:, :HD]
        build[r, 2:4] = asked[:, HD:]
        build[r, 4:6] = tokens[2 * r : 2 * r + 2, :HD]
        build[r, 6:8] = tokens[2 * r : 2 * r + 2, HD:]
        length = lens[r]
        build[r, 8:9] = jnp.full((1, HD), (length >> 7) * PAGE, jnp.int32).astype(F32)
        build[r, 9:10] = jnp.full((1, HD), length & (PAGE - 1), jnp.int32).astype(F32)
        packet = build[r].astype(BF16)
        mine[r] = packet
        pack[home] = packet


def layer_kernel(
    table, kv, pack, mine, w, res, gain,
    recv, upd, nrm,
    kvv, wv, res_win, res32, sbuf, pkt, qs, nks, nvs, lens, score,
    part, land1, half1, half2, land2, relay, back, back_out, back_in, hid, sq_own, sq_all,
    load_sem, page_send, page_recv, pkt_send, pkt_recv, back_send, back_recv,
    rs_send, rs_recv, sq_send, sq_recv,
):
    g = lax.axis_index("group")
    t = lax.axis_index("tp")
    parity = lax.rem(t, 2)
    get_kv = pltpu.make_async_copy(kv, kvv, load_sem.at[0])
    get_w = pltpu.make_async_copy(w, wv, load_sem.at[1])
    get_res = pltpu.make_async_copy(
        res.at[:, :, pl.ds(pl.multiple_of((t // 2) * 640, 128), 640)], res_win, load_sem.at[2]
    )
    get_kv.start()
    get_w.start()
    get_res.start()

    def at_z(o):
        return lax.rem(t + (o + NT), NT)

    barrier = pltpu.get_barrier_semaphore()

    def greet_group(k, carry):
        pl.semaphore_signal(
            barrier, inc=1, device_id=(group_ahead(g, k), t), device_id_type=MESH
        )
        return carry

    def greet_tp(k, carry):
        pl.semaphore_signal(
            barrier, inc=1, device_id=(g, lax.rem(t + k, NT)), device_id_type=MESH
        )
        return carry

    lax.fori_loop(1, NG, greet_group, 0)
    lax.fori_loop(1, NT, greet_tp, 0)
    pl.semaphore_wait(barrier, NG + NT - 2)

    def packet_copy(k):
        d = group_ahead(g, k)
        return pltpu.make_async_remote_copy(
            src_ref=pack.at[d], dst_ref=pkt.at[g],
            send_sem=pkt_send.at[k], recv_sem=pkt_recv.at[g],
            device_id=(d, t), device_id_type=MESH,
        )

    def packet_here(k):
        s = group_behind(g, k)
        return pltpu.make_async_remote_copy(
            src_ref=pack.at[s], dst_ref=pkt.at[s],
            send_sem=pkt_send.at[k], recv_sem=pkt_recv.at[s],
            device_id=(group_ahead(g, k), t), device_id_type=MESH,
        )

    def send_packet(k, carry):
        packet_copy(k).start()
        return carry

    def take_packet(k, carry):
        packet_here(k).wait()
        return carry

    lax.fori_loop(1, NG, send_packet, 0)
    get_kv.wait()

    offsets = torus_offsets()

    core = lax.rem(g, 2)

    def page_copy(n, landed):
        hops, ky, kx, kc = offsets[n]
        d = group_at(g, ky + core * (4 - 2 * ky), kx + core * (4 - 2 * kx), kc)
        back = 1 - core if kc == 0 else core
        s = group_at(g, ky + back * (4 - 2 * ky), kx + back * (4 - 2 * kx), kc) if landed else g
        return d, pltpu.make_async_remote_copy(
            src_ref=sbuf.at[n], dst_ref=recv.at[s],
            send_sem=page_send.at[n], recv_sem=page_recv.at[s],
            device_id=(d, t), device_id_type=MESH,
        )

    def send_pages(first, last):
        for n in range(first, last):
            d, copy = page_copy(n, False)
            sbuf[n] = kvv[table[SLOT_TO + d]]
            copy.start()

    send_pages(0, 3)

    get_res.wait()
    res32[...] = jnp.zeros_like(res32)
    for a in range(ROWS):
        res32[2 * a : 2 * a + 2, :] = res_win[a].astype(F32)
    qs[...] = jnp.zeros_like(qs)
    nks[...] = jnp.zeros_like(nks)
    nvs[...] = jnp.zeros_like(nvs)
    lens[...] = jnp.zeros_like(lens)
    lax.fori_loop(1, NG, take_packet, 0)
    send_pages(3, 6)

    for i in range(ROWS):
        at = table[B_SRC + i]
        stay = table[B_STAY + i]
        near = mine[at * stay].astype(F32)
        far = pkt[at * (1 - stay)].astype(F32)
        row = jnp.where(stay == 1, near, far)
        qs[2 * i : 2 * i + 2, :] = row[0:2]
        qs[RP + 2 * i : RP + 2 * i + 2, :] = row[2:4]
        nks[2 * i : 2 * i + 2, :] = row[4:6]
        nvs[2 * i : 2 * i + 2, :] = row[6:8]
        length = jnp.broadcast_to(row[8:9] + row[9:10], (2, HD))
        lens[2 * i : 2 * i + 2, :] = length
        lens[RP + 2 * i : RP + 2 * i + 2, :] = length

    qa = qs[...].astype(BF16)
    row_all = lax.broadcasted_iota(jnp.int32, (2 * RP, PAGE), 0) & (RP - 1)
    lane = lax.broadcasted_iota(jnp.int32, (2 * RP, PAGE), 1)
    row_b = row_all >> 1
    lane_f = lane.astype(F32)
    row_len = lens[...]
    sc = lax.dot_general(
        qa, nks[...].astype(BF16), (((1,), (1,)), ((), ())), preferred_element_type=F32
    ) * (HD**-0.5)
    sc = jnp.where(((lane >> 1) == row_b) & ((lane & 1) <= (row_all & 1)), sc, -1e30)
    score[SLOTS] = sc
    top = sc
    for c in range(SLOTS):
        sc = lax.dot_general(
            qa, kvv[c, :, :HD], (((1,), (1,)), ((), ())), preferred_element_type=F32
        ) * (HD**-0.5)
        pos = lane_f + (table[NUM + c] * PAGE).astype(F32)
        sc = jnp.where((row_b == table[OWN + c]) & (pos < row_len), sc, -1e30)
        score[c] = sc
        top = jnp.maximum(top, sc)
    send_pages(6, 9)
    top = jnp.max(top, axis=1, keepdims=True)
    weight = jnp.exp(score[SLOTS] - top)
    total = weight
    mixed = jnp.dot(weight.astype(BF16), nvs[...].astype(BF16), preferred_element_type=F32)
    for c in range(SLOTS):
        weight = jnp.exp(score[c] - top)
        total = total + weight
        mixed = mixed + jnp.dot(
            weight.astype(BF16), kvv[c, :, HD:], preferred_element_type=F32
        )
    mixed = mixed / jnp.sum(total, axis=1, keepdims=True)
    att = jnp.concatenate([mixed[:RP], mixed[RP:]], axis=1).astype(BF16)

    get_w.wait()
    send_pages(9, 11)
    low = lax.broadcasted_iota(jnp.int32, (16, 128), 1) < 64
    for i in range(NT // 2):
        out = jnp.dot(att, wv[:, 640 * i : 640 * i + 640], preferred_element_type=F32)
        mid = out[:, 256:384]
        part[2 * i, 0:32] = out[:, 0:128].astype(BF16)
        part[2 * i, 32:64] = out[:, 128:256].astype(BF16)
        part[2 * i, 64:80] = jnp.where(low, mid[:16], pltpu.roll(mid[16:], 64, 1)).astype(BF16)
        part[2 * i + 1, 0:32] = out[:, 384:512].astype(BF16)
        part[2 * i + 1, 32:64] = out[:, 512:640].astype(BF16)
        part[2 * i + 1, 64:80] = jnp.where(
            low, pltpu.roll(mid[:16], 64, 1), mid[16:]
        ).astype(BF16)

    def z_copy(n, src, dst, o):
        return pltpu.make_async_remote_copy(
            src_ref=src, dst_ref=dst, send_sem=rs_send.at[n], recv_sem=rs_recv.at[n],
            device_id=(g, at_z(o)), device_id_type=MESH,
        )

    first = {
        1: z_copy(1, part.at[at_z(-7)], land1.at[1], -2),
        5: z_copy(5, part.at[at_z(7)], land1.at[5], 2),
        8: z_copy(8, part.at[at_z(8), pl.ds(0, 48)], half1, -3),
        9: z_copy(9, part.at[at_z(8), pl.ds(48, 32)], half2, 3),
        0: z_copy(0, part.at[at_z(-6)], land1.at[0], -1),
        4: z_copy(4, part.at[at_z(6)], land1.at[4], 1),
        3: z_copy(3, part.at[at_z(-4)], land1.at[3], -2),
        7: z_copy(7, part.at[at_z(4)], land1.at[7], 2),
        2: z_copy(2, part.at[at_z(-3)], land1.at[2], -1),
        6: z_copy(6, part.at[at_z(3)], land1.at[6], 1),
        10: z_copy(10, part.at[at_z(-1)], land2.at[0], -1),
        11: z_copy(11, part.at[at_z(1)], land2.at[1], 1),
    }
    for copy in first.values():
        copy.start()
    send_pages(11, 15)
    second = [
        z_copy(12, relay.at[0], land2.at[2], -5),
        z_copy(13, relay.at[1], land2.at[3], 5),
        z_copy(14, relay.at[2], land2.at[4], -2),
        z_copy(15, relay.at[3], land2.at[5], 2),
    ]
    for n, o, a, b in ((2, -2, 2, 3), (3, 2, 6, 7)):
        first[a].wait_recv()
        first[b].wait_recv()
        relay[n] = (
            part[at_z(o)].astype(F32) + land1[a].astype(F32) + land1[b].astype(F32)
        ).astype(BF16)
        second[n].start()
    send_pages(15, 19)
    for n, o, a, b, c in ((0, -5, 0, 1, 8), (1, 5, 4, 5, 9)):
        first[a].wait_recv()
        first[b].wait_recv()
        first[c].wait_recv()
        whole = part[at_z(o)].astype(F32) + land1[a].astype(F32) + land1[b].astype(F32)
        if n == 0:
            relay[n, 0:48] = (whole[0:48] + half1[...].astype(F32)).astype(BF16)
            relay[n, 48:80] = whole[48:80].astype(BF16)
        else:
            relay[n, 0:48] = whole[0:48].astype(BF16)
            relay[n, 48:80] = (whole[48:80] + half2[...].astype(F32)).astype(BF16)
        second[n].start()
    send_pages(19, 23)
    acc = part[t].astype(F32)
    first[10].wait_recv()
    first[11].wait_recv()
    acc = acc + land2[0].astype(F32) + land2[1].astype(F32)
    for n in (2, 3, 0, 1):
        second[n].wait_recv()
        acc = acc + land2[2 + n].astype(F32)

    back[...] = jnp.zeros_like(back)
    tail = jnp.concatenate([acc[64:80], pltpu.roll(acc[64:80], 64, 1)], axis=0)
    for i in range(ROWS):
        back[i, 0:2] = acc[2 * i : 2 * i + 2]
        back[i, 2:4] = acc[32 + 2 * i : 34 + 2 * i]
        back[i, 4:6] = tail[2 * i : 2 * i + 2]

    def back_copy(k):
        d = group_ahead(g, k)
        return d, pltpu.make_async_remote_copy(
            src_ref=back_out.at[d], dst_ref=back_in.at[g],
            send_sem=back_send.at[k], recv_sem=back_recv.at[g],
            device_id=(d, t), device_id_type=MESH,
        )

    def send_back(k, carry):
        d, copy = back_copy(k)
        back_out[d] = back[table[RET_SRC + d]]
        copy.start()
        return carry

    def take_back(k, carry):
        s = group_behind(g, k)
        pltpu.make_async_remote_copy(
            src_ref=back_out.at[s], dst_ref=back_in.at[s],
            send_sem=back_send.at[k], recv_sem=back_recv.at[s],
            device_id=(group_ahead(g, k), t), device_id_type=MESH,
        ).wait()
        return carry

    lax.fori_loop(1, NG, send_back, 0)
    send_pages(23, 27)

    hid[...] = jnp.zeros_like(hid)
    lax.fori_loop(1, NG, take_back, 0)
    for r in range(ROWS):
        at = table[A_SRC + r]
        stay = table[A_STAY + r]
        row = jnp.where(stay == 1, back[at * stay], back_in[at * (1 - stay)])
        for j in range(3):
            hid[j, 2 * r : 2 * r + 2, :] = row[2 * j : 2 * j + 2]

    even = parity == 0
    mid = res32[:, 256:384]
    sum_a = hid[0] + jnp.where(even, res32[:, 0:128], res32[:, 384:512])
    sum_b = hid[1] + jnp.where(even, res32[:, 128:256], res32[:, 512:640])
    sum_h = hid[2] + jnp.where(even, mid, pltpu.roll(mid, 64, 1))
    own = lax.broadcasted_iota(jnp.int32, (RP, 128), 1) < 64
    sum_h = jnp.where(own, sum_h, 0.0)
    square = jnp.sum(sum_a * sum_a + sum_b * sum_b + sum_h * sum_h, axis=1, keepdims=True)
    diag = lax.broadcasted_iota(jnp.int32, (RP, 128), 0) == lax.broadcasted_iota(
        jnp.int32, (RP, 128), 1
    )
    sq_own[...] = jnp.sum(jnp.where(diag, square, 0.0), axis=0, keepdims=True)

    def square_copy(k):
        return pltpu.make_async_remote_copy(
            src_ref=sq_own, dst_ref=sq_all.at[k],
            send_sem=sq_send.at[k], recv_sem=sq_recv.at[k],
            device_id=(g, at_z(k)), device_id_type=MESH,
        )

    order = [8, 7, 9, 6, 10, 5, 11, 4, 12, 3, 13, 2, 14, 1, 15]
    for k in order:
        square_copy(k).start()
    send_pages(27, 31)
    tail = sum_h[:, 0:64]
    value = jnp.where(
        even,
        jnp.concatenate([sum_a, sum_b, tail], axis=1),
        jnp.concatenate([tail, sum_a, sum_b], axis=1),
    )
    for a in range(ROWS):
        upd[a] = value[2 * a : 2 * a + 2, :].astype(BF16)
    scaled = value * gain[...].astype(F32).reshape(1, COLS)
    whole = sq_own[...]
    for k in reversed(order):
        square_copy(k).wait()
        whole = whole + sq_all[k]
    inverse = lax.rsqrt(whole * (1.0 / D) + 1e-6)
    factor = jnp.sum(jnp.where(diag, inverse, 0.0), axis=1, keepdims=True)
    scaled = scaled * factor
    for a in range(ROWS):
        nrm[a] = scaled[2 * a : 2 * a + 2, :].astype(BF16)

    for copy in first.values():
        copy.wait_send()
    for copy in second:
        copy.wait_send()
    for n in range(NG - 1):
        page_copy(n, True)[1].wait()


def place_kernel(
    table, lens, pb, pa, kv, recv, fresh, upd_in, nrm_in, kva, upd, nrm, buf, page_sem, out_sem
):
    def fetch(r, carry):
        need = (lens[r] + (STEPS + PAGE - 1)) >> 7
        at = table[A_SRC + r]
        stay = table[A_STAY + r]
        for j in range(4):
            @pl.when((j < need) & (stay == 0))
            def _():
                c = pa[j, r]
                pltpu.make_async_copy(recv.at[at], buf.at[c], page_sem.at[c]).start()

            @pl.when((j < need) & (stay == 1))
            def _():
                c = pa[j, r]
                pltpu.make_async_copy(kv.at[pb[j, at]], buf.at[c], page_sem.at[c]).start()
        return carry

    lax.fori_loop(0, ROWS, fetch, 0)
    upd[...] = upd_in[...]
    nrm[...] = nrm_in[...]
    lane_row = lax.broadcasted_iota(jnp.int32, (16, 2 * HD), 0)
    for c in range(SLOTS):
        pltpu.make_async_copy(kv.at[0], buf.at[c], page_sem.at[c]).wait()

    def write(r, carry):
        for s in range(STEPS):
            p = lens[r] + s
            c = pa[p >> 7, r]
            e = p & (PAGE - 1)
            base = pl.multiple_of((e >> 4) << 4, 16)
            block = buf[c, pl.ds(base, 16), :].astype(F32)
            token = fresh[pl.ds(2 * r + s, 1), :]
            buf[c, pl.ds(base, 16), :] = jnp.where(
                lane_row == (e & 15), token, block
            ).astype(BF16)
        return carry

    lax.fori_loop(0, ROWS, write, 0)
    out = pltpu.make_async_copy(buf, kva, out_sem)
    out.start()
    out.wait()


VM = pl.BlockSpec(memory_space=pltpu.VMEM)
SM = pl.BlockSpec(memory_space=pltpu.SMEM)
HBM = pl.BlockSpec(memory_space=pltpu.HBM)
DMA = pltpu.SemaphoreType.DMA


def on_device(
    lengths, destination, page_before, page_after, kv_cache,
    queries, new_kv, residual, out_weight, norm_gain,
):
    kv = kv_cache[0, 0]
    pb, pa = page_before.T, page_after.T
    table, pack, mine, fresh = pl.pallas_call(
        route_kernel,
        out_shape=(
            jax.ShapeDtypeStruct((TABLE,), jnp.int32),
            jax.ShapeDtypeStruct((NG, 16, 128), BF16),
            jax.ShapeDtypeStruct((16, 16, 128), BF16),
            jax.ShapeDtypeStruct((RP, 2 * HD), F32),
        ),
        in_specs=[HBM] * 5,
        out_specs=(SM, VM, VM, VM),
        scratch_shapes=[
            pltpu.SMEM((ROWS,), jnp.int32),
            pltpu.SMEM((NG * ROWS,), jnp.int32),
            pltpu.SMEM((4, ROWS), jnp.int32),
            pltpu.VMEM((ROWS, STEPS, 2 * HD), BF16),
            pltpu.VMEM((STEPS, ROWS, 8, 2 * HD), BF16),
            pltpu.SMEM((ROWS + 1,), jnp.int32),
            pltpu.VMEM((ROWS, 16, 128), F32),
            DMA((5,)),
        ],
        compiler_params=pltpu.CompilerParams(vmem_limit_bytes=60 << 20),
        name="route",
    )(lengths, destination, pb, queries.transpose(1, 0, 2), new_kv)
    recv, upd, nrm = pl.pallas_call(
        layer_kernel,
        out_shape=(
            jax.ShapeDtypeStruct((NG, PAGE, 2 * HD), BF16),
            jax.ShapeDtypeStruct((ROWS, STEPS, COLS), BF16),
            jax.ShapeDtypeStruct((ROWS, STEPS, COLS), BF16),
        ),
        in_specs=[SM, HBM, HBM, VM, HBM, HBM, VM],
        out_specs=(HBM, VM, VM),
        scratch_shapes=[
            pltpu.VMEM((SLOTS, PAGE, 2 * HD), BF16),
            pltpu.VMEM((2 * HD, D), BF16),
            pltpu.VMEM((ROWS, STEPS, 640), BF16),
            pltpu.VMEM((RP, 640), F32),
            pltpu.VMEM((NG, PAGE, 2 * HD), BF16),
            pltpu.VMEM((NG, 16, 128), BF16),
            pltpu.VMEM((2 * RP, HD), F32),
            pltpu.VMEM((128, HD), F32),
            pltpu.VMEM((128, HD), F32),
            pltpu.VMEM((2 * RP, HD), F32),
            pltpu.VMEM((SLOTS + 1, 2 * RP, PAGE), F32),
            pltpu.VMEM((NT, BLK, 128), BF16),
            pltpu.VMEM((8, BLK, 128), BF16),
            pltpu.VMEM((48, 128), BF16),
            pltpu.VMEM((32, 128), BF16),
            pltpu.VMEM((6, BLK, 128), BF16),
            pltpu.VMEM((4, BLK, 128), BF16),
            pltpu.VMEM((16, 8, 128), F32),
            pltpu.VMEM((NG, 8, 128), F32),
            pltpu.VMEM((NG, 8, 128), F32),
            pltpu.VMEM((3, RP, 128), F32),
            pltpu.VMEM((1, 128), F32),
            pltpu.VMEM((NT, 1, 128), F32),
            DMA((3,)),
            DMA((NG,)),
            DMA((NG,)),
            DMA((NG,)),
            DMA((NG,)),
            DMA((NG,)),
            DMA((NG,)),
            DMA((16,)),
            DMA((16,)),
            DMA((NT,)),
            DMA((NT,)),
        ],
        compiler_params=pltpu.CompilerParams(
            collective_id=0, has_side_effects=True, vmem_limit_bytes=58 << 20
        ),
        name="layer",
    )(
        table, kv, pack, mine, out_weight, residual.transpose(1, 0, 2),
        norm_gain,
    )
    kva, upd, nrm = pl.pallas_call(
        place_kernel,
        out_shape=(
            jax.ShapeDtypeStruct((SLOTS, PAGE, 2 * HD), BF16),
            jax.ShapeDtypeStruct((ROWS, STEPS, COLS), BF16),
            jax.ShapeDtypeStruct((ROWS, STEPS, COLS), BF16),
        ),
        in_specs=[SM, SM, SM, SM, HBM, HBM, VM, VM, VM],
        out_specs=(HBM, VM, VM),
        scratch_shapes=[
            pltpu.VMEM((SLOTS, PAGE, 2 * HD), BF16),
            DMA((SLOTS,)),
            DMA(()),
        ],
        compiler_params=pltpu.CompilerParams(vmem_limit_bytes=60 << 20),
        name="place",
    )(table, lengths, pb, pa, kv, recv, fresh, upd, nrm)
    return kva[None, None], upd.transpose(1, 0, 2), nrm.transpose(1, 0, 2)


def solution(mesh):
    in_specs = (
        P("group"),
        P(),
        P("group", None),
        P("group", None),
        P("group", "tp", None, None, None),
        P(None, "group", "tp"),
        P(None, "group", None, None),
        P(None, "group", None),
        P("tp", None),
        P("tp"),
    )
    out_specs = (P("group", "tp", None, None, None), P(None, "group", "tp"), P(None, "group", "tp"))
    return jax.shard_map(
        on_device, mesh=mesh, in_specs=in_specs, out_specs=out_specs, check_vma=False
    )
```

```python
import jax
import jax.numpy as jnp
from jax import lax
from jax.experimental import pallas as pl
from jax.experimental.pallas import tpu as pltpu
from jax.sharding import PartitionSpec as P

MESH = pl.DeviceIdType.MESH
NG = 32
NT = 16
ROWS = 13
STEPS = 2
SLOTS = 16
PAGE = 128
HD = 128
RP = 32
D = 5120
COLS = D // NT
BLK = 80
F32 = jnp.float32
BF16 = jnp.bfloat16

SLOT_TO, RET_SRC, B_SRC, B_STAY, OWN, NUM, A_SRC, A_STAY = 0, 32, 64, 80, 96, 112, 128, 144
A_POS, ARRIVED = 160, 176
TABLE = 192
MOVED = 11
HALF = PAGE // 2


def torus_offsets():
    found = []
    for ky in range(4):
        for kx in range(4):
            for kc in range(2):
                if (ky, kx, kc) != (0, 0, 0):
                    found.append((min(ky, 4 - ky) + min(kx, 4 - kx), ky, kx, kc))
    return sorted(found, key=lambda o: -o[0])


def route_kernel(
    lens_in, dest_in, pb_in, q_in, nkv_in, table, pack, mine, fresh,
    lens, dest, pb, q, nkv, anchor, build, sem,
):
    loads = [
        pltpu.make_async_copy(src, dst, sem.at[n])
        for n, (src, dst) in enumerate(
            ((dest_in, dest), (lens_in, lens), (pb_in, pb), (nkv_in, nkv), (q_in, q))
        )
    ]
    for load in loads:
        load.start()
    pack[...] = jnp.zeros_like(pack)
    build[...] = jnp.zeros_like(build)
    for load in loads:
        load.wait()
    g = lax.axis_index("group")
    head = lax.axis_index("tp") // 2
    base = g * ROWS

    def scan(b, carry):
        r = dest[b] - base
        anchor[jnp.where((r >= 0) & (r < ROWS), r, ROWS)] = b
        return carry

    lax.fori_loop(0, NG * ROWS, scan, 0, unroll=16)

    def clear(d, carry):
        table[SLOT_TO + d] = 0
        table[RET_SRC + d] = 0
        return carry

    lax.fori_loop(0, NG, clear, 0, unroll=8)

    def before(i, carry):
        to = dest[base + i]
        r = to - base
        stay = (r >= 0) & (r < ROWS)
        d = to // ROWS
        table[SLOT_TO + d] = pb[0, i]
        table[RET_SRC + d] = i
        table[B_SRC + i] = jnp.where(stay, r, d)
        table[B_STAY + i] = stay.astype(jnp.int32)
        length = lens[jnp.where(stay, r, 0)]
        need = jnp.where(stay, (length + (STEPS + PAGE - 1)) >> 7, 1)
        for j in range(4):
            @pl.when(j < need)
            def _():
                c = pb[j, i]
                table[OWN + c] = i
                table[NUM + c] = j
        return carry

    lax.fori_loop(0, ROWS, before, 0)

    rid = lax.broadcasted_iota(jnp.int32, (RP, 208), 0)
    cid = lax.broadcasted_iota(jnp.int32, (RP, 208), 1)
    pick = (cid == ((rid & 1) * ROWS + (rid >> 1)) * 8 + head) & (rid < STEPS * ROWS)
    tokens = jnp.dot(
        pick.astype(F32).astype(BF16),
        nkv[...].astype(F32).reshape(208, 2 * HD).astype(BF16),
        preferred_element_type=F32,
    )
    fresh[...] = tokens
    count = 0
    for r in range(ROWS):
        anc = anchor[r]
        loc = anc - base
        stay = (loc >= 0) & (loc < ROWS)
        home = anc // ROWS
        table[A_SRC + r] = jnp.where(stay, loc, home)
        table[A_STAY + r] = stay.astype(jnp.int32)
        table[A_POS + r] = count
        table[ARRIVED + count] = home
        count = count + jnp.where(stay, 0, 1)
        asked = q[r].astype(F32)
        build[r, 0:2] = asked[:, :HD]
        build[r, 2:4] = asked[:, HD:]
        build[r, 4:6] = tokens[2 * r : 2 * r + 2, :HD]
        build[r, 6:8] = tokens[2 * r : 2 * r + 2, HD:]
        length = lens[r]
        build[r, 8:9] = jnp.full((1, HD), (length >> 7) * PAGE, jnp.int32).astype(F32)
        build[r, 9:10] = jnp.full((1, HD), length & (PAGE - 1), jnp.int32).astype(F32)
        packet = build[r].astype(BF16)
        mine[r] = packet
        pack[home] = packet


def layer_kernel(
    table, kv, pack, mine, w, res, gain,
    moved, upd, nrm,
    kvv, wv, res_win, res32, sbuf, recv, comp, pkt, qs, nks, nvs, lens, score,
    part, land1, half1, half2, land2, relay, back, back_out, back_in, hid, sq_own, sq_all,
    load_sem, keep_sem, swap_send, swap_recv, page_send, page_recv, pkt_send, pkt_recv, back_send, back_recv,
    rs_send, rs_recv, sq_send, sq_recv,
):
    g = lax.axis_index("group")
    t = lax.axis_index("tp")
    parity = lax.rem(t, 2)
    get_kv = pltpu.make_async_copy(kv, kvv, load_sem.at[0])
    get_w = pltpu.make_async_copy(w, wv, load_sem.at[1])
    get_res = pltpu.make_async_copy(
        res.at[:, :, pl.ds(pl.multiple_of((t // 2) * 640, 128), 640)], res_win, load_sem.at[2]
    )
    get_kv.start()
    get_w.start()
    get_res.start()

    zs = [lax.rem(t + o, NT) for o in range(NT)]

    def at_z(o):
        return zs[o % NT]

    core, x, y = lax.rem(g, 2), lax.rem(g // 2, 4), g // 8
    ys = [lax.rem(y + k, 4) * 8 for k in range(4)]
    xs = [lax.rem(x + k, 4) * 2 for k in range(4)]
    cs = [core, 1 - core]
    ys_to = [ys[k] + core * (ys[-k % 4] - ys[k]) for k in range(4)]
    xs_to = [xs[k] + core * (xs[-k % 4] - xs[k]) for k in range(4)]
    offsets = torus_offsets()
    peers = [ys_to[ky] + xs_to[kx] + cs[kc] for _, ky, kx, kc in offsets]

    barrier = pltpu.get_barrier_semaphore()
    for d in peers:
        pl.semaphore_signal(barrier, inc=1, device_id=(d, t), device_id_type=MESH)
    for o in range(1, NT):
        pl.semaphore_signal(barrier, inc=1, device_id=(g, zs[o]), device_id_type=MESH)
    pl.semaphore_wait(barrier, NG + NT - 2)

    def group_copy(src, dst, send_sem, recv_sem, d):
        return pltpu.make_async_remote_copy(
            src_ref=src, dst_ref=dst, send_sem=send_sem, recv_sem=recv_sem,
            device_id=(d, t), device_id_type=MESH,
        )

    def all_copies(src, dst, send_sem, recv_sem):
        most = pl.ds(0, NG - 1)
        return group_copy(src.at[most], dst.at[most], send_sem, recv_sem, peers[0])

    for d in peers:
        group_copy(pack.at[d], pkt.at[g], pkt_send, pkt_recv, d).start()
    packets = all_copies(pack, pkt, pkt_send, pkt_recv)
    get_kv.wait()

    half = pl.ds(pl.multiple_of(parity * HALF, HALF), HALF)

    def send_pages(first, last):
        for n in range(first, last):
            d = peers[n]
            sbuf[n] = kvv[table[SLOT_TO + d], half, :]
            group_copy(sbuf.at[n], recv.at[g], page_send, page_recv, d).start()

    send_pages(0, 4)

    get_res.wait()
    res32[...] = jnp.zeros_like(res32)
    for a in range(ROWS):
        res32[2 * a : 2 * a + 2, :] = res_win[a].astype(F32)
    qs[...] = jnp.zeros_like(qs)
    nks[...] = jnp.zeros_like(nks)
    nvs[...] = jnp.zeros_like(nvs)
    lens[...] = jnp.zeros_like(lens)
    packets.wait_recv()
    send_pages(4, 8)

    for i in range(ROWS):
        at = table[B_SRC + i]
        stay = table[B_STAY + i]
        near = mine[at * stay].astype(F32)
        far = pkt[at * (1 - stay)].astype(F32)
        row = jnp.where(stay == 1, near, far)
        qs[2 * i : 2 * i + 2, :] = row[0:2]
        qs[RP + 2 * i : RP + 2 * i + 2, :] = row[2:4]
        nks[2 * i : 2 * i + 2, :] = row[4:6]
        nvs[2 * i : 2 * i + 2, :] = row[6:8]
        length = jnp.broadcast_to(row[8:9] + row[9:10], (2, HD))
        lens[2 * i : 2 * i + 2, :] = length
        lens[RP + 2 * i : RP + 2 * i + 2, :] = length

    qa = qs[...].astype(BF16)
    row_all = lax.broadcasted_iota(jnp.int32, (2 * RP, PAGE), 0) & (RP - 1)
    lane = lax.broadcasted_iota(jnp.int32, (2 * RP, PAGE), 1)
    row_b = row_all >> 1
    lane_f = lane.astype(F32)
    row_len = lens[...]
    sc = lax.dot_general(
        qa, nks[...].astype(BF16), (((1,), (1,)), ((), ())), preferred_element_type=F32
    ) * (HD**-0.5)
    sc = jnp.where(((lane >> 1) == row_b) & ((lane & 1) <= (row_all & 1)), sc, -1e30)
    score[SLOTS] = sc
    top = sc
    for c in range(SLOTS):
        sc = lax.dot_general(
            qa, kvv[c, :, :HD], (((1,), (1,)), ((), ())), preferred_element_type=F32
        ) * (HD**-0.5)
        pos = lane_f + (table[NUM + c] * PAGE).astype(F32)
        sc = jnp.where((row_b == table[OWN + c]) & (pos < row_len), sc, -1e30)
        score[c] = sc
        top = jnp.maximum(top, sc)
    send_pages(8, 13)
    top = jnp.max(top, axis=1, keepdims=True)
    weight = jnp.exp(score[SLOTS] - top)
    total = weight
    mixed = jnp.dot(weight.astype(BF16), nvs[...].astype(BF16), preferred_element_type=F32)
    for c in range(SLOTS):
        weight = jnp.exp(score[c] - top)
        total = total + weight
        mixed = mixed + jnp.dot(
            weight.astype(BF16), kvv[c, :, HD:], preferred_element_type=F32
        )
    mixed = mixed / jnp.sum(total, axis=1, keepdims=True)
    att = jnp.concatenate([mixed[:RP], mixed[RP:]], axis=1).astype(BF16)

    get_w.wait()
    send_pages(13, 17)
    low = lax.broadcasted_iota(jnp.int32, (16, 128), 1) < 64
    for i in range(NT // 2):
        out = jnp.dot(att, wv[:, 640 * i : 640 * i + 640], preferred_element_type=F32)
        mid = out[:, 256:384]
        part[2 * i, 0:32] = out[:, 0:128].astype(BF16)
        part[2 * i, 32:64] = out[:, 128:256].astype(BF16)
        part[2 * i, 64:80] = jnp.where(low, mid[:16], pltpu.roll(mid[16:], 64, 1)).astype(BF16)
        part[2 * i + 1, 0:32] = out[:, 384:512].astype(BF16)
        part[2 * i + 1, 32:64] = out[:, 512:640].astype(BF16)
        part[2 * i + 1, 64:80] = jnp.where(
            low, pltpu.roll(mid[:16], 64, 1), mid[16:]
        ).astype(BF16)

    def z_copy(n, src, dst, o):
        return pltpu.make_async_remote_copy(
            src_ref=src, dst_ref=dst, send_sem=rs_send.at[n], recv_sem=rs_recv.at[n],
            device_id=(g, at_z(o)), device_id_type=MESH,
        )

    first = {
        1: z_copy(1, part.at[at_z(-7)], land1.at[1], -2),
        5: z_copy(5, part.at[at_z(7)], land1.at[5], 2),
        8: z_copy(8, part.at[at_z(8), pl.ds(0, 48)], half1, -3),
        9: z_copy(9, part.at[at_z(8), pl.ds(48, 32)], half2, 3),
        0: z_copy(0, part.at[at_z(-6)], land1.at[0], -1),
        4: z_copy(4, part.at[at_z(6)], land1.at[4], 1),
        3: z_copy(3, part.at[at_z(-4)], land1.at[3], -2),
        7: z_copy(7, part.at[at_z(4)], land1.at[7], 2),
        2: z_copy(2, part.at[at_z(-3)], land1.at[2], -1),
        6: z_copy(6, part.at[at_z(3)], land1.at[6], 1),
        10: z_copy(10, part.at[at_z(-1)], land2.at[0], -1),
        11: z_copy(11, part.at[at_z(1)], land2.at[1], 1),
    }
    for copy in first.values():
        copy.start()
    send_pages(17, 24)
    second = [
        z_copy(12, relay.at[0], land2.at[2], -5),
        z_copy(13, relay.at[1], land2.at[3], 5),
        z_copy(14, relay.at[2], land2.at[4], -2),
        z_copy(15, relay.at[3], land2.at[5], 2),
    ]
    for n, o, a, b in ((2, -2, 2, 3), (3, 2, 6, 7)):
        first[a].wait_recv()
        first[b].wait_recv()
        relay[n] = (
            part[at_z(o)].astype(F32) + land1[a].astype(F32) + land1[b].astype(F32)
        ).astype(BF16)
        second[n].start()
    send_pages(24, 31)
    for n, o, a, b, c in ((0, -5, 0, 1, 8), (1, 5, 4, 5, 9)):
        first[a].wait_recv()
        first[b].wait_recv()
        first[c].wait_recv()
        whole = part[at_z(o)].astype(F32) + land1[a].astype(F32) + land1[b].astype(F32)
        if n == 0:
            relay[n, 0:48] = (whole[0:48] + half1[...].astype(F32)).astype(BF16)
            relay[n, 48:80] = whole[48:80].astype(BF16)
        else:
            relay[n, 0:48] = whole[0:48].astype(BF16)
            relay[n, 48:80] = (whole[48:80] + half2[...].astype(F32)).astype(BF16)
        second[n].start()
    pages = all_copies(sbuf, recv, page_send, page_recv)
    pages.wait_recv()
    for j in range(MOVED):
        comp[j] = recv[table[ARRIVED + j]]

    def swap_copy(n, first, count):
        some = pl.ds(first, count)
        return pltpu.make_async_remote_copy(
            src_ref=comp.at[some], dst_ref=moved.at[some, half],
            send_sem=swap_send.at[n], recv_sem=swap_recv.at[n],
            device_id=(g, t + 1 - 2 * parity), device_id_type=MESH,
        )

    swaps = [swap_copy(0, 0, 6), swap_copy(1, 6, MOVED - 6)]
    swaps[0].start()
    keep = pltpu.make_async_copy(comp, moved.at[:, half], keep_sem)
    keep.start()
    acc = part[t].astype(F32)
    first[10].wait_recv()
    first[11].wait_recv()
    acc = acc + land2[0].astype(F32) + land2[1].astype(F32)
    for n in (2, 3, 0, 1):
        second[n].wait_recv()
        acc = acc + land2[2 + n].astype(F32)

    back[...] = jnp.zeros_like(back)
    tail = jnp.concatenate([acc[64:80], pltpu.roll(acc[64:80], 64, 1)], axis=0)
    for i in range(ROWS):
        back[i, 0:2] = acc[2 * i : 2 * i + 2]
        back[i, 2:4] = acc[32 + 2 * i : 34 + 2 * i]
        back[i, 4:6] = tail[2 * i : 2 * i + 2]

    for d in peers:
        back_out[d] = back[table[RET_SRC + d]]
        group_copy(back_out.at[d], back_in.at[g], back_send, back_recv, d).start()
    returns = all_copies(back_out, back_in, back_send, back_recv)
    swaps[1].start()

    hid[...] = jnp.zeros_like(hid)
    returns.wait_recv()
    for r in range(ROWS):
        at = table[A_SRC + r]
        stay = table[A_STAY + r]
        row = jnp.where(stay == 1, back[at * stay], back_in[at * (1 - stay)])
        for j in range(3):
            hid[j, 2 * r : 2 * r + 2, :] = row[2 * j : 2 * j + 2]

    even = parity == 0
    mid = res32[:, 256:384]
    sum_a = hid[0] + jnp.where(even, res32[:, 0:128], res32[:, 384:512])
    sum_b = hid[1] + jnp.where(even, res32[:, 128:256], res32[:, 512:640])
    sum_h = hid[2] + jnp.where(even, mid, pltpu.roll(mid, 64, 1))
    own = lax.broadcasted_iota(jnp.int32, (RP, 128), 1) < 64
    sum_h = jnp.where(own, sum_h, 0.0)
    square = jnp.sum(sum_a * sum_a + sum_b * sum_b + sum_h * sum_h, axis=1, keepdims=True)
    diag = lax.broadcasted_iota(jnp.int32, (RP, 128), 0) == lax.broadcasted_iota(
        jnp.int32, (RP, 128), 1
    )
    sq_own[...] = jnp.sum(jnp.where(diag, square, 0.0), axis=0, keepdims=True)

    for o in (8, 7, 9, 6, 10, 5, 11, 4, 12, 3, 13, 2, 14, 1, 15):
        pltpu.make_async_remote_copy(
            src_ref=sq_own, dst_ref=sq_all.at[o], send_sem=sq_send, recv_sem=sq_recv,
            device_id=(g, zs[o]), device_id_type=MESH,
        ).start()
    most = pl.ds(1, NT - 1)
    squares = pltpu.make_async_remote_copy(
        src_ref=sq_all.at[most], dst_ref=sq_all.at[most], send_sem=sq_send, recv_sem=sq_recv,
        device_id=(g, zs[1]), device_id_type=MESH,
    )
    tail = sum_h[:, 0:64]
    value = jnp.where(
        even,
        jnp.concatenate([sum_a, sum_b, tail], axis=1),
        jnp.concatenate([tail, sum_a, sum_b], axis=1),
    )
    for a in range(ROWS):
        upd[a] = value[2 * a : 2 * a + 2, :].astype(BF16)
    scaled = value * gain[...].astype(F32).reshape(1, COLS)
    whole = sq_own[...]
    squares.wait_recv()
    for k in range(1, NT):
        whole = whole + sq_all[k]
    inverse = lax.rsqrt(whole * (1.0 / D) + 1e-6)
    factor = jnp.sum(jnp.where(diag, inverse, 0.0), axis=1, keepdims=True)
    scaled = scaled * factor
    for a in range(ROWS):
        nrm[a] = scaled[2 * a : 2 * a + 2, :].astype(BF16)

    for copy in first.values():
        copy.wait_send()
    for copy in second:
        copy.wait_send()
    packets.wait_send()
    returns.wait_send()
    squares.wait_send()
    pages.wait_send()
    keep.wait()
    for copy in swaps:
        copy.wait()


def place_kernel(
    table, lens, pb, pa, kv, moved, fresh, upd_in, nrm_in, kva, upd, nrm, buf, page_sem, out_sem
):
    passed = [
        pltpu.make_async_copy(upd_in, upd, out_sem.at[1]),
        pltpu.make_async_copy(nrm_in, nrm, out_sem.at[2]),
    ]
    for copy in passed:
        copy.start()

    def fetch(r, carry):
        need = (lens[r] + (STEPS + PAGE - 1)) >> 7
        at = table[A_SRC + r]
        pos = table[A_POS + r]
        stay = table[A_STAY + r]
        for j in range(4):
            @pl.when((j < need) & (stay == 0))
            def _():
                c = pa[j, r]
                pltpu.make_async_copy(moved.at[pos], buf.at[c], page_sem.at[c]).start()

            @pl.when((j < need) & (stay == 1))
            def _():
                c = pa[j, r]
                pltpu.make_async_copy(kv.at[pb[j, at]], buf.at[c], page_sem.at[c]).start()
        return carry

    lax.fori_loop(0, ROWS, fetch, 0)
    lane_row = lax.broadcasted_iota(jnp.int32, (16, 2 * HD), 0)
    for c in range(SLOTS):
        pltpu.make_async_copy(kv.at[0], buf.at[c], page_sem.at[c]).wait()

    def write(r, carry):
        for s in range(STEPS):
            p = lens[r] + s
            c = pa[p >> 7, r]
            e = p & (PAGE - 1)
            base = pl.multiple_of((e >> 4) << 4, 16)
            block = buf[c, pl.ds(base, 16), :].astype(F32)
            token = fresh[pl.ds(2 * r + s, 1), :]
            buf[c, pl.ds(base, 16), :] = jnp.where(
                lane_row == (e & 15), token, block
            ).astype(BF16)
        return carry

    lax.fori_loop(0, ROWS, write, 0)
    out = pltpu.make_async_copy(buf, kva, out_sem.at[0])
    out.start()
    for copy in passed:
        copy.wait()
    out.wait()


VM = pl.BlockSpec(memory_space=pltpu.VMEM)
SM = pl.BlockSpec(memory_space=pltpu.SMEM)
HBM = pl.BlockSpec(memory_space=pltpu.HBM)
DMA = pltpu.SemaphoreType.DMA


def on_device(
    lengths, destination, page_before, page_after, kv_cache,
    queries, new_kv, residual, out_weight, norm_gain,
):
    kv = kv_cache[0, 0]
    pb, pa = page_before.T, page_after.T
    table, pack, mine, fresh = pl.pallas_call(
        route_kernel,
        out_shape=(
            jax.ShapeDtypeStruct((TABLE,), jnp.int32),
            jax.ShapeDtypeStruct((NG, 16, 128), BF16),
            jax.ShapeDtypeStruct((16, 16, 128), BF16),
            jax.ShapeDtypeStruct((RP, 2 * HD), F32),
        ),
        in_specs=[HBM] * 5,
        out_specs=(SM, VM, VM, VM),
        scratch_shapes=[
            pltpu.SMEM((ROWS,), jnp.int32),
            pltpu.SMEM((NG * ROWS,), jnp.int32),
            pltpu.SMEM((4, ROWS), jnp.int32),
            pltpu.VMEM((ROWS, STEPS, 2 * HD), BF16),
            pltpu.VMEM((STEPS, ROWS, 8, 2 * HD), BF16),
            pltpu.SMEM((ROWS + 1,), jnp.int32),
            pltpu.VMEM((ROWS, 16, 128), F32),
            DMA((5,)),
        ],
        compiler_params=pltpu.CompilerParams(vmem_limit_bytes=60 << 20),
        name="route",
    )(lengths, destination, pb, queries.transpose(1, 0, 2), new_kv)
    moved, upd, nrm = pl.pallas_call(
        layer_kernel,
        out_shape=(
            jax.ShapeDtypeStruct((MOVED, PAGE, 2 * HD), BF16),
            jax.ShapeDtypeStruct((ROWS, STEPS, COLS), BF16),
            jax.ShapeDtypeStruct((ROWS, STEPS, COLS), BF16),
        ),
        in_specs=[SM, HBM, HBM, VM, HBM, HBM, VM],
        out_specs=(HBM, VM, VM),
        scratch_shapes=[
            pltpu.VMEM((SLOTS, PAGE, 2 * HD), BF16),
            pltpu.VMEM((2 * HD, D), BF16),
            pltpu.VMEM((ROWS, STEPS, 640), BF16),
            pltpu.VMEM((RP, 640), F32),
            pltpu.VMEM((NG, HALF, 2 * HD), BF16),
            pltpu.VMEM((NG, HALF, 2 * HD), BF16),
            pltpu.VMEM((MOVED, HALF, 2 * HD), BF16),
            pltpu.VMEM((NG, 16, 128), BF16),
            pltpu.VMEM((2 * RP, HD), F32),
            pltpu.VMEM((128, HD), F32),
            pltpu.VMEM((128, HD), F32),
            pltpu.VMEM((2 * RP, HD), F32),
            pltpu.VMEM((SLOTS + 1, 2 * RP, PAGE), F32),
            pltpu.VMEM((NT, BLK, 128), BF16),
            pltpu.VMEM((8, BLK, 128), BF16),
            pltpu.VMEM((48, 128), BF16),
            pltpu.VMEM((32, 128), BF16),
            pltpu.VMEM((6, BLK, 128), BF16),
            pltpu.VMEM((4, BLK, 128), BF16),
            pltpu.VMEM((16, 8, 128), F32),
            pltpu.VMEM((NG, 8, 128), F32),
            pltpu.VMEM((NG, 8, 128), F32),
            pltpu.VMEM((3, RP, 128), F32),
            pltpu.VMEM((1, 128), F32),
            pltpu.VMEM((NT, 1, 128), F32),
            DMA((3,)),
            DMA(()),
            DMA((2,)),
            DMA((2,)),
            DMA(()),
            DMA(()),
            DMA(()),
            DMA(()),
            DMA(()),
            DMA(()),
            DMA((16,)),
            DMA((16,)),
            DMA(()),
            DMA(()),
        ],
        compiler_params=pltpu.CompilerParams(
            collective_id=0, has_side_effects=True, vmem_limit_bytes=58 << 20
        ),
        name="layer",
    )(
        table, kv, pack, mine, out_weight, residual.transpose(1, 0, 2),
        norm_gain,
    )
    kva, upd, nrm = pl.pallas_call(
        place_kernel,
        out_shape=(
            jax.ShapeDtypeStruct((SLOTS, PAGE, 2 * HD), BF16),
            jax.ShapeDtypeStruct((ROWS, STEPS, COLS), BF16),
            jax.ShapeDtypeStruct((ROWS, STEPS, COLS), BF16),
        ),
        in_specs=[SM, SM, SM, SM, HBM, HBM, VM, HBM, HBM],
        out_specs=(HBM, HBM, HBM),
        scratch_shapes=[
            pltpu.VMEM((SLOTS, PAGE, 2 * HD), BF16),
            DMA((SLOTS,)),
            DMA((3,)),
        ],
        compiler_params=pltpu.CompilerParams(vmem_limit_bytes=60 << 20),
        name="place",
    )(table, lengths, pb, pa, kv, moved, fresh, upd, nrm)
    return kva[None, None], upd.transpose(1, 0, 2), nrm.transpose(1, 0, 2)


def solution(mesh):
    in_specs = (
        P("group"),
        P(),
        P("group", None),
        P("group", None),
        P("group", "tp", None, None, None),
        P(None, "group", "tp"),
        P(None, "group", None, None),
        P(None, "group", None),
        P("tp", None),
        P("tp"),
    )
    out_specs = (P("group", "tp", None, None, None), P(None, "group", "tp"), P(None, "group", "tp"))
    return jax.shard_map(
        on_device, mesh=mesh, in_specs=in_specs, out_specs=out_specs, check_vma=False
    )
```

```python
import jax
import jax.numpy as jnp
from jax import lax
from jax.experimental import pallas as pl
from jax.experimental.pallas import tpu as pltpu
from jax.sharding import PartitionSpec as P

MESH = pl.DeviceIdType.MESH
NG = 32
NT = 16
ROWS = 13
STEPS = 2
SLOTS = 16
PAGE = 128
HD = 128
RP = 32
D = 5120
COLS = D // NT
BLK = 80
F32 = jnp.float32
BF16 = jnp.bfloat16

SLOT_TO, RET_SRC, B_SRC, B_STAY, OWN, NUM, A_SRC, A_STAY = 0, 32, 64, 80, 96, 112, 128, 144
A_POS, ARRIVED = 160, 176
TABLE = 192
MOVED = 11
HALF = PAGE // 2


def torus_offsets():
    found = []
    for ky in range(4):
        for kx in range(4):
            for kc in range(2):
                if (ky, kx, kc) != (0, 0, 0):
                    found.append((min(ky, 4 - ky) + min(kx, 4 - kx), ky, kx, kc))
    return sorted(found, key=lambda o: -o[0])


def route_kernel(
    lens_in, dest_in, pb_in, q_in, nkv_in, table, pack, mine, fresh,
    lens, dest, pb, q, nkv, anchor, build, sem,
):
    loads = [
        pltpu.make_async_copy(src, dst, sem.at[n])
        for n, (src, dst) in enumerate(
            ((dest_in, dest), (lens_in, lens), (pb_in, pb), (nkv_in, nkv), (q_in, q))
        )
    ]
    for load in loads:
        load.start()
    pack[...] = jnp.zeros_like(pack)
    build[...] = jnp.zeros_like(build)
    for load in loads:
        load.wait()
    g = lax.axis_index("group")
    head = lax.axis_index("tp") // 2
    base = g * ROWS

    def scan(b, carry):
        r = dest[b] - base
        anchor[jnp.where((r >= 0) & (r < ROWS), r, ROWS)] = b
        return carry

    lax.fori_loop(0, NG * ROWS, scan, 0, unroll=16)

    def clear(d, carry):
        table[SLOT_TO + d] = 0
        table[RET_SRC + d] = 0
        return carry

    lax.fori_loop(0, NG, clear, 0, unroll=8)

    def before(i, carry):
        to = dest[base + i]
        r = to - base
        stay = (r >= 0) & (r < ROWS)
        d = to // ROWS
        table[SLOT_TO + d] = pb[0, i]
        table[RET_SRC + d] = i
        table[B_SRC + i] = jnp.where(stay, r, d)
        table[B_STAY + i] = stay.astype(jnp.int32)
        length = lens[jnp.where(stay, r, 0)]
        need = jnp.where(stay, (length + (STEPS + PAGE - 1)) >> 7, 1)
        for j in range(4):
            @pl.when(j < need)
            def _():
                c = pb[j, i]
                table[OWN + c] = i
                table[NUM + c] = j
        return carry

    lax.fori_loop(0, ROWS, before, 0)

    rid = lax.broadcasted_iota(jnp.int32, (RP, 208), 0)
    cid = lax.broadcasted_iota(jnp.int32, (RP, 208), 1)
    pick = (cid == ((rid & 1) * ROWS + (rid >> 1)) * 8 + head) & (rid < STEPS * ROWS)
    tokens = jnp.dot(
        pick.astype(F32).astype(BF16),
        nkv[...].astype(F32).reshape(208, 2 * HD).astype(BF16),
        preferred_element_type=F32,
    )
    fresh[...] = tokens
    count = 0
    for r in range(ROWS):
        anc = anchor[r]
        loc = anc - base
        stay = (loc >= 0) & (loc < ROWS)
        home = anc // ROWS
        table[A_SRC + r] = jnp.where(stay, loc, home)
        table[A_STAY + r] = stay.astype(jnp.int32)
        table[A_POS + r] = count
        table[ARRIVED + count] = home
        count = count + jnp.where(stay, 0, 1)
        asked = q[r].astype(F32)
        build[r, 0:2] = asked[:, :HD]
        build[r, 2:4] = asked[:, HD:]
        build[r, 4:6] = tokens[2 * r : 2 * r + 2, :HD]
        build[r, 6:8] = tokens[2 * r : 2 * r + 2, HD:]
        length = lens[r]
        build[r, 8:9] = jnp.full((1, HD), (length >> 7) * PAGE, jnp.int32).astype(F32)
        build[r, 9:10] = jnp.full((1, HD), length & (PAGE - 1), jnp.int32).astype(F32)
        packet = build[r].astype(BF16)
        mine[r] = packet
        pack[home] = packet


def layer_kernel(
    table, kv, pack, mine, w, res, gain,
    moved, upd, nrm,
    kvv, wv, res_win, res32, sbuf, recv, comp, pkt, qs, nks, nvs, lens, score,
    part, land1, half1, half2, land2, relay, back, back_out, back_in, hid, sq_own, sq_all,
    load_sem, keep_sem, swap_send, swap_recv, page_send, page_recv, pkt_send, pkt_recv, back_send, back_recv,
    rs_send, rs_recv, sq_send, sq_recv,
):
    g = lax.axis_index("group")
    t = lax.axis_index("tp")
    parity = lax.rem(t, 2)
    get_kv = pltpu.make_async_copy(kv, kvv, load_sem.at[0])
    get_w = pltpu.make_async_copy(w, wv, load_sem.at[1])
    get_res = pltpu.make_async_copy(
        res.at[:, :, pl.ds(pl.multiple_of((t // 2) * 640, 128), 640)], res_win, load_sem.at[2]
    )
    get_kv.start()
    get_w.start()
    get_res.start()

    zs = [lax.rem(t + o, NT) for o in range(NT)]

    def at_z(o):
        return zs[o % NT]

    core, x, y = lax.rem(g, 2), lax.rem(g // 2, 4), g // 8
    ys = [lax.rem(y + k, 4) * 8 for k in range(4)]
    xs = [lax.rem(x + k, 4) * 2 for k in range(4)]
    cs = [core, 1 - core]
    ys_to = [ys[k] + core * (ys[-k % 4] - ys[k]) for k in range(4)]
    xs_to = [xs[k] + core * (xs[-k % 4] - xs[k]) for k in range(4)]
    offsets = torus_offsets()
    peers = [ys_to[ky] + xs_to[kx] + cs[kc] for _, ky, kx, kc in offsets]

    barrier = pltpu.get_barrier_semaphore()
    for d in peers:
        pl.semaphore_signal(barrier, inc=1, device_id=(d, t), device_id_type=MESH)
    for o in range(1, NT):
        pl.semaphore_signal(barrier, inc=1, device_id=(g, zs[o]), device_id_type=MESH)
    pl.semaphore_wait(barrier, NG + NT - 2)

    def group_copy(src, dst, send_sem, recv_sem, d):
        return pltpu.make_async_remote_copy(
            src_ref=src, dst_ref=dst, send_sem=send_sem, recv_sem=recv_sem,
            device_id=(d, t), device_id_type=MESH,
        )

    def all_copies(src, dst, send_sem, recv_sem):
        most = pl.ds(0, NG - 1)
        return group_copy(src.at[most], dst.at[most], send_sem, recv_sem, peers[0])

    for d in peers:
        group_copy(pack.at[d], pkt.at[g], pkt_send, pkt_recv, d).start()
    packets = all_copies(pack, pkt, pkt_send, pkt_recv)
    get_kv.wait()

    half = pl.ds(pl.multiple_of(parity * HALF, HALF), HALF)

    def send_pages(first, last):
        for n in range(first, last):
            d = peers[n]
            sbuf[n] = kvv[table[SLOT_TO + d], half, :]
            group_copy(sbuf.at[n], recv.at[g], page_send, page_recv, d).start()

    send_pages(0, 4)

    get_res.wait()
    res32[...] = jnp.zeros_like(res32)
    for a in range(ROWS):
        res32[2 * a : 2 * a + 2, :] = res_win[a].astype(F32)
    qs[...] = jnp.zeros_like(qs)
    nks[...] = jnp.zeros_like(nks)
    nvs[...] = jnp.zeros_like(nvs)
    lens[...] = jnp.zeros_like(lens)
    packets.wait_recv()
    send_pages(4, 8)

    for i in range(ROWS):
        at = table[B_SRC + i]
        stay = table[B_STAY + i]
        near = mine[at * stay].astype(F32)
        far = pkt[at * (1 - stay)].astype(F32)
        row = jnp.where(stay == 1, near, far)
        qs[2 * i : 2 * i + 2, :] = row[0:2]
        qs[RP + 2 * i : RP + 2 * i + 2, :] = row[2:4]
        nks[2 * i : 2 * i + 2, :] = row[4:6]
        nvs[2 * i : 2 * i + 2, :] = row[6:8]
        length = jnp.broadcast_to(row[8:9] + row[9:10], (2, HD))
        lens[2 * i : 2 * i + 2, :] = length
        lens[RP + 2 * i : RP + 2 * i + 2, :] = length

    qa = qs[...].astype(BF16)
    row_all = lax.broadcasted_iota(jnp.int32, (2 * RP, PAGE), 0) & (RP - 1)
    lane = lax.broadcasted_iota(jnp.int32, (2 * RP, PAGE), 1)
    row_b = row_all >> 1
    lane_f = lane.astype(F32)
    row_len = lens[...]
    sc = lax.dot_general(
        qa, nks[...].astype(BF16), (((1,), (1,)), ((), ())), preferred_element_type=F32
    ) * (HD**-0.5)
    sc = jnp.where(((lane >> 1) == row_b) & ((lane & 1) <= (row_all & 1)), sc, -1e30)
    score[SLOTS] = sc
    top = sc
    for c in range(SLOTS):
        sc = lax.dot_general(
            qa, kvv[c, :, :HD], (((1,), (1,)), ((), ())), preferred_element_type=F32
        ) * (HD**-0.5)
        pos = lane_f + (table[NUM + c] * PAGE).astype(F32)
        sc = jnp.where((row_b == table[OWN + c]) & (pos < row_len), sc, -1e30)
        score[c] = sc
        top = jnp.maximum(top, sc)
    send_pages(8, 13)
    top = jnp.max(top, axis=1, keepdims=True)
    weight = jnp.exp(score[SLOTS] - top)
    total = weight
    mixed = jnp.dot(weight.astype(BF16), nvs[...].astype(BF16), preferred_element_type=F32)
    for c in range(SLOTS):
        weight = jnp.exp(score[c] - top)
        total = total + weight
        mixed = mixed + jnp.dot(
            weight.astype(BF16), kvv[c, :, HD:], preferred_element_type=F32
        )
    mixed = mixed / jnp.sum(total, axis=1, keepdims=True)
    att = jnp.concatenate([mixed[:RP], mixed[RP:]], axis=1).astype(BF16)

    get_w.wait()
    send_pages(13, 17)
    low = lax.broadcasted_iota(jnp.int32, (16, 128), 1) < 64

    def project(m):
        pair = lax.rem(t // 2 + m, NT // 2)
        columns = pl.ds(pl.multiple_of(pair * 640, 128), 640)
        out = jnp.dot(att, wv[:, columns], preferred_element_type=F32)
        mid = out[:, 256:384]
        left, right = 2 * pair, 2 * pair + 1
        part[left, 0:32] = out[:, 0:128].astype(BF16)
        part[left, 32:64] = out[:, 128:256].astype(BF16)
        part[left, 64:80] = jnp.where(low, mid[:16], pltpu.roll(mid[16:], 64, 1)).astype(BF16)
        part[right, 0:32] = out[:, 384:512].astype(BF16)
        part[right, 32:64] = out[:, 512:640].astype(BF16)
        part[right, 64:80] = jnp.where(low, pltpu.roll(mid[:16], 64, 1), mid[16:]).astype(BF16)

    def z_copy(n, src, dst, o):
        return pltpu.make_async_remote_copy(
            src_ref=src, dst_ref=dst, send_sem=rs_send.at[n], recv_sem=rs_recv.at[n],
            device_id=(g, at_z(o)), device_id_type=MESH,
        )

    first = {
        1: z_copy(1, part.at[at_z(-7)], land1.at[1], -2),
        5: z_copy(5, part.at[at_z(7)], land1.at[5], 2),
        8: z_copy(8, part.at[at_z(8), pl.ds(0, 48)], half1, -3),
        9: z_copy(9, part.at[at_z(8), pl.ds(48, 32)], half2, 3),
        0: z_copy(0, part.at[at_z(-6)], land1.at[0], -1),
        4: z_copy(4, part.at[at_z(6)], land1.at[4], 1),
        3: z_copy(3, part.at[at_z(-4)], land1.at[3], -2),
        7: z_copy(7, part.at[at_z(4)], land1.at[7], 2),
        2: z_copy(2, part.at[at_z(-3)], land1.at[2], -1),
        6: z_copy(6, part.at[at_z(3)], land1.at[6], 1),
        10: z_copy(10, part.at[at_z(-1)], land2.at[0], -1),
        11: z_copy(11, part.at[at_z(1)], land2.at[1], 1),
    }
    for pairs, ready in (((4, 3, 5), (1, 5, 8, 9, 0, 4)), ((2, 6, 1, 7), (3, 7, 2, 6)), ((0,), (10, 11))):
        for m in pairs:
            project(m)
        for n in ready:
            first[n].start()
    send_pages(17, 24)
    second = [
        z_copy(12, relay.at[0], land2.at[2], -5),
        z_copy(13, relay.at[1], land2.at[3], 5),
        z_copy(14, relay.at[2], land2.at[4], -2),
        z_copy(15, relay.at[3], land2.at[5], 2),
    ]
    for n, o, a, b, c in ((0, -5, 0, 1, 8), (1, 5, 4, 5, 9)):
        first[a].wait_recv()
        first[b].wait_recv()
        first[c].wait_recv()
        whole = part[at_z(o)].astype(F32) + land1[a].astype(F32) + land1[b].astype(F32)
        if n == 0:
            relay[n, 0:48] = (whole[0:48] + half1[...].astype(F32)).astype(BF16)
            relay[n, 48:80] = whole[48:80].astype(BF16)
        else:
            relay[n, 0:48] = whole[0:48].astype(BF16)
            relay[n, 48:80] = (whole[48:80] + half2[...].astype(F32)).astype(BF16)
        second[n].start()
    for n, o, a, b in ((2, -2, 2, 3), (3, 2, 6, 7)):
        first[a].wait_recv()
        first[b].wait_recv()
        relay[n] = (
            part[at_z(o)].astype(F32) + land1[a].astype(F32) + land1[b].astype(F32)
        ).astype(BF16)
        second[n].start()
    send_pages(24, 31)
    acc = part[t].astype(F32)
    first[10].wait_recv()
    first[11].wait_recv()
    acc = acc + land2[0].astype(F32) + land2[1].astype(F32)
    for n in (2, 3):
        second[n].wait_recv()
        acc = acc + land2[2 + n].astype(F32)

    pages = all_copies(sbuf, recv, page_send, page_recv)
    pages.wait_recv()
    for j in range(MOVED):
        comp[j] = recv[table[ARRIVED + j]]

    def swap_copy(n, first, count):
        some = pl.ds(first, count)
        return pltpu.make_async_remote_copy(
            src_ref=comp.at[some], dst_ref=moved.at[some, half],
            send_sem=swap_send.at[n], recv_sem=swap_recv.at[n],
            device_id=(g, t + 1 - 2 * parity), device_id_type=MESH,
        )

    swaps = [swap_copy(0, 0, 3), swap_copy(1, 3, 4), swap_copy(2, 7, 4)]
    swaps[0].start()
    keep = pltpu.make_async_copy(comp, moved.at[:, half], keep_sem)
    keep.start()
    for n in (0, 1):
        second[n].wait_recv()
        acc = acc + land2[2 + n].astype(F32)

    back[...] = jnp.zeros_like(back)
    tail = jnp.concatenate([acc[64:80], pltpu.roll(acc[64:80], 64, 1)], axis=0)
    for i in range(ROWS):
        back[i, 0:2] = acc[2 * i : 2 * i + 2]
        back[i, 2:4] = acc[32 + 2 * i : 34 + 2 * i]
        back[i, 4:6] = tail[2 * i : 2 * i + 2]

    for d in peers:
        back_out[d] = back[table[RET_SRC + d]]
        group_copy(back_out.at[d], back_in.at[g], back_send, back_recv, d).start()
    returns = all_copies(back_out, back_in, back_send, back_recv)
    swaps[1].start()

    hid[...] = jnp.zeros_like(hid)
    returns.wait_recv()
    for r in range(ROWS):
        at = table[A_SRC + r]
        stay = table[A_STAY + r]
        row = jnp.where(stay == 1, back[at * stay], back_in[at * (1 - stay)])
        for j in range(3):
            hid[j, 2 * r : 2 * r + 2, :] = row[2 * j : 2 * j + 2]

    even = parity == 0
    mid = res32[:, 256:384]
    sum_a = hid[0] + jnp.where(even, res32[:, 0:128], res32[:, 384:512])
    sum_b = hid[1] + jnp.where(even, res32[:, 128:256], res32[:, 512:640])
    sum_h = hid[2] + jnp.where(even, mid, pltpu.roll(mid, 64, 1))
    own = lax.broadcasted_iota(jnp.int32, (RP, 128), 1) < 64
    sum_h = jnp.where(own, sum_h, 0.0)
    square = jnp.sum(sum_a * sum_a + sum_b * sum_b + sum_h * sum_h, axis=1, keepdims=True)
    diag = lax.broadcasted_iota(jnp.int32, (RP, 128), 0) == lax.broadcasted_iota(
        jnp.int32, (RP, 128), 1
    )
    sq_own[...] = jnp.sum(jnp.where(diag, square, 0.0), axis=0, keepdims=True)

    for o in (8, 7, 9, 6, 10, 5, 11, 4, 12, 3, 13, 2, 14, 1, 15):
        pltpu.make_async_remote_copy(
            src_ref=sq_own, dst_ref=sq_all.at[o], send_sem=sq_send, recv_sem=sq_recv,
            device_id=(g, zs[o]), device_id_type=MESH,
        ).start()
    swaps[2].start()
    most = pl.ds(1, NT - 1)
    squares = pltpu.make_async_remote_copy(
        src_ref=sq_all.at[most], dst_ref=sq_all.at[most], send_sem=sq_send, recv_sem=sq_recv,
        device_id=(g, zs[1]), device_id_type=MESH,
    )
    tail = sum_h[:, 0:64]
    value = jnp.where(
        even,
        jnp.concatenate([sum_a, sum_b, tail], axis=1),
        jnp.concatenate([tail, sum_a, sum_b], axis=1),
    )
    for a in range(ROWS):
        upd[a] = value[2 * a : 2 * a + 2, :].astype(BF16)
    scaled = value * gain[...].astype(F32).reshape(1, COLS)
    whole = sq_own[...]
    squares.wait_recv()
    for k in range(1, NT):
        whole = whole + sq_all[k]
    inverse = lax.rsqrt(whole * (1.0 / D) + 1e-6)
    factor = jnp.sum(jnp.where(diag, inverse, 0.0), axis=1, keepdims=True)
    scaled = scaled * factor
    for a in range(ROWS):
        nrm[a] = scaled[2 * a : 2 * a + 2, :].astype(BF16)

    for copy in first.values():
        copy.wait_send()
    for copy in second:
        copy.wait_send()
    packets.wait_send()
    returns.wait_send()
    squares.wait_send()
    pages.wait_send()
    keep.wait()
    for copy in swaps:
        copy.wait()


def place_kernel(
    table, lens, pb, pa, kv, moved, fresh, upd_in, nrm_in, kva, upd, nrm, buf, page_sem, out_sem
):
    passed = [
        pltpu.make_async_copy(upd_in, upd, out_sem.at[1]),
        pltpu.make_async_copy(nrm_in, nrm, out_sem.at[2]),
    ]
    for copy in passed:
        copy.start()

    def fetch(r, carry):
        need = (lens[r] + (STEPS + PAGE - 1)) >> 7
        at = table[A_SRC + r]
        pos = table[A_POS + r]
        stay = table[A_STAY + r]
        for j in range(4):
            @pl.when((j < need) & (stay == 0))
            def _():
                c = pa[j, r]
                pltpu.make_async_copy(moved.at[pos], buf.at[c], page_sem.at[c]).start()

            @pl.when((j < need) & (stay == 1))
            def _():
                c = pa[j, r]
                pltpu.make_async_copy(kv.at[pb[j, at]], buf.at[c], page_sem.at[c]).start()
        return carry

    lax.fori_loop(0, ROWS, fetch, 0)
    lane_row = lax.broadcasted_iota(jnp.int32, (16, 2 * HD), 0)
    for c in range(SLOTS):
        pltpu.make_async_copy(kv.at[0], buf.at[c], page_sem.at[c]).wait()

    def write(r, carry):
        for s in range(STEPS):
            p = lens[r] + s
            c = pa[p >> 7, r]
            e = p & (PAGE - 1)
            base = pl.multiple_of((e >> 4) << 4, 16)
            block = buf[c, pl.ds(base, 16), :].astype(F32)
            token = fresh[pl.ds(2 * r + s, 1), :]
            buf[c, pl.ds(base, 16), :] = jnp.where(
                lane_row == (e & 15), token, block
            ).astype(BF16)
        return carry

    lax.fori_loop(0, ROWS, write, 0)
    out = pltpu.make_async_copy(buf, kva, out_sem.at[0])
    out.start()
    for copy in passed:
        copy.wait()
    out.wait()


VM = pl.BlockSpec(memory_space=pltpu.VMEM)
SM = pl.BlockSpec(memory_space=pltpu.SMEM)
HBM = pl.BlockSpec(memory_space=pltpu.HBM)
DMA = pltpu.SemaphoreType.DMA


def on_device(
    lengths, destination, page_before, page_after, kv_cache,
    queries, new_kv, residual, out_weight, norm_gain,
):
    kv = kv_cache[0, 0]
    pb, pa = page_before.T, page_after.T
    table, pack, mine, fresh = pl.pallas_call(
        route_kernel,
        out_shape=(
            jax.ShapeDtypeStruct((TABLE,), jnp.int32),
            jax.ShapeDtypeStruct((NG, 16, 128), BF16),
            jax.ShapeDtypeStruct((16, 16, 128), BF16),
            jax.ShapeDtypeStruct((RP, 2 * HD), F32),
        ),
        in_specs=[HBM] * 5,
        out_specs=(SM, VM, VM, VM),
        scratch_shapes=[
            pltpu.SMEM((ROWS,), jnp.int32),
            pltpu.SMEM((NG * ROWS,), jnp.int32),
            pltpu.SMEM((4, ROWS), jnp.int32),
            pltpu.VMEM((ROWS, STEPS, 2 * HD), BF16),
            pltpu.VMEM((STEPS, ROWS, 8, 2 * HD), BF16),
            pltpu.SMEM((ROWS + 1,), jnp.int32),
            pltpu.VMEM((ROWS, 16, 128), F32),
            DMA((5,)),
        ],
        compiler_params=pltpu.CompilerParams(vmem_limit_bytes=60 << 20),
        name="route",
    )(lengths, destination, pb, queries.transpose(1, 0, 2), new_kv)
    moved, upd, nrm = pl.pallas_call(
        layer_kernel,
        out_shape=(
            jax.ShapeDtypeStruct((MOVED, PAGE, 2 * HD), BF16),
            jax.ShapeDtypeStruct((ROWS, STEPS, COLS), BF16),
            jax.ShapeDtypeStruct((ROWS, STEPS, COLS), BF16),
        ),
        in_specs=[SM, HBM, HBM, VM, HBM, HBM, VM],
        out_specs=(HBM, VM, VM),
        scratch_shapes=[
            pltpu.VMEM((SLOTS, PAGE, 2 * HD), BF16),
            pltpu.VMEM((2 * HD, D), BF16),
            pltpu.VMEM((ROWS, STEPS, 640), BF16),
            pltpu.VMEM((RP, 640), F32),
            pltpu.VMEM((NG, HALF, 2 * HD), BF16),
            pltpu.VMEM((NG, HALF, 2 * HD), BF16),
            pltpu.VMEM((MOVED, HALF, 2 * HD), BF16),
            pltpu.VMEM((NG, 16, 128), BF16),
            pltpu.VMEM((2 * RP, HD), F32),
            pltpu.VMEM((128, HD), F32),
            pltpu.VMEM((128, HD), F32),
            pltpu.VMEM((2 * RP, HD), F32),
            pltpu.VMEM((SLOTS + 1, 2 * RP, PAGE), F32),
            pltpu.VMEM((NT, BLK, 128), BF16),
            pltpu.VMEM((8, BLK, 128), BF16),
            pltpu.VMEM((48, 128), BF16),
            pltpu.VMEM((32, 128), BF16),
            pltpu.VMEM((6, BLK, 128), BF16),
            pltpu.VMEM((4, BLK, 128), BF16),
            pltpu.VMEM((16, 8, 128), F32),
            pltpu.VMEM((NG, 8, 128), F32),
            pltpu.VMEM((NG, 8, 128), F32),
            pltpu.VMEM((3, RP, 128), F32),
            pltpu.VMEM((1, 128), F32),
            pltpu.VMEM((NT, 1, 128), F32),
            DMA((3,)),
            DMA(()),
            DMA((3,)),
            DMA((3,)),
            DMA(()),
            DMA(()),
            DMA(()),
            DMA(()),
            DMA(()),
            DMA(()),
            DMA((16,)),
            DMA((16,)),
            DMA(()),
            DMA(()),
        ],
        compiler_params=pltpu.CompilerParams(
            collective_id=0, has_side_effects=True, vmem_limit_bytes=58 << 20
        ),
        name="layer",
    )(
        table, kv, pack, mine, out_weight, residual.transpose(1, 0, 2),
        norm_gain,
    )
    kva, upd, nrm = pl.pallas_call(
        place_kernel,
        out_shape=(
            jax.ShapeDtypeStruct((SLOTS, PAGE, 2 * HD), BF16),
            jax.ShapeDtypeStruct((ROWS, STEPS, COLS), BF16),
            jax.ShapeDtypeStruct((ROWS, STEPS, COLS), BF16),
        ),
        in_specs=[SM, SM, SM, SM, HBM, HBM, VM, HBM, HBM],
        out_specs=(HBM, HBM, HBM),
        scratch_shapes=[
            pltpu.VMEM((SLOTS, PAGE, 2 * HD), BF16),
            DMA((SLOTS,)),
            DMA((3,)),
        ],
        compiler_params=pltpu.CompilerParams(vmem_limit_bytes=60 << 20),
        name="place",
    )(table, lengths, pb, pa, kv, moved, fresh, upd, nrm)
    return kva[None, None], upd.transpose(1, 0, 2), nrm.transpose(1, 0, 2)


def solution(mesh):
    in_specs = (
        P("group"),
        P(),
        P("group", None),
        P("group", None),
        P("group", "tp", None, None, None),
        P(None, "group", "tp"),
        P(None, "group", None, None),
        P(None, "group", None),
        P("tp", None),
        P("tp"),
    )
    out_specs = (P("group", "tp", None, None, None), P(None, "group", "tp"), P(None, "group", "tp"))
    return jax.shard_map(
        on_device, mesh=mesh, in_specs=in_specs, out_specs=out_specs, check_vma=False
    )
```

```python
import jax
import jax.numpy as jnp
from jax import lax
from jax.experimental import pallas as pl
from jax.experimental.pallas import tpu as pltpu
from jax.sharding import PartitionSpec as P

MESH = pl.DeviceIdType.MESH
NG = 32
NT = 16
ROWS = 13
STEPS = 2
SLOTS = 16
PAGE = 128
HD = 128
RP = 32
D = 5120
COLS = D // NT
BLK = 80
F32 = jnp.float32
BF16 = jnp.bfloat16

SLOT_TO, RET_SRC, B_SRC, B_STAY, OWN, NUM, A_SRC, A_STAY = 0, 32, 64, 80, 96, 112, 128, 144
A_POS, ARRIVED = 160, 176
TABLE = 192
MOVED = 11
HALF = 48
REST = PAGE - 2 * HALF


def torus_offsets():
    found = []
    for ky in range(4):
        for kx in range(4):
            for kc in range(2):
                if (ky, kx, kc) != (0, 0, 0):
                    found.append((min(ky, 4 - ky) + min(kx, 4 - kx), ky, kx, kc))
    return sorted(found, key=lambda o: -o[0])


def route_kernel(
    lens_in, dest_in, pb_in, q_in, nkv_in, table, pack, mine, fresh,
    lens, dest, pb, q, nkv, anchor, build, sem,
):
    loads = [
        pltpu.make_async_copy(src, dst, sem.at[n])
        for n, (src, dst) in enumerate(
            ((dest_in, dest), (lens_in, lens), (pb_in, pb), (nkv_in, nkv), (q_in, q))
        )
    ]
    for load in loads:
        load.start()
    pack[...] = jnp.zeros_like(pack)
    build[...] = jnp.zeros_like(build)
    for load in loads:
        load.wait()
    g = lax.axis_index("group")
    head = lax.axis_index("tp") // 2
    base = g * ROWS

    def scan(b, carry):
        r = dest[b] - base
        anchor[jnp.where((r >= 0) & (r < ROWS), r, ROWS)] = b
        return carry

    lax.fori_loop(0, NG * ROWS, scan, 0, unroll=16)

    def clear(d, carry):
        table[SLOT_TO + d] = 0
        table[RET_SRC + d] = 0
        return carry

    lax.fori_loop(0, NG, clear, 0, unroll=8)

    def before(i, carry):
        to = dest[base + i]
        r = to - base
        stay = (r >= 0) & (r < ROWS)
        d = to // ROWS
        table[SLOT_TO + d] = pb[0, i]
        table[RET_SRC + d] = i
        table[B_SRC + i] = jnp.where(stay, r, d)
        table[B_STAY + i] = stay.astype(jnp.int32)
        length = lens[jnp.where(stay, r, 0)]
        need = jnp.where(stay, (length + (STEPS + PAGE - 1)) >> 7, 1)
        for j in range(4):
            @pl.when(j < need)
            def _():
                c = pb[j, i]
                table[OWN + c] = i
                table[NUM + c] = j
        return carry

    lax.fori_loop(0, ROWS, before, 0)

    rid = lax.broadcasted_iota(jnp.int32, (RP, 208), 0)
    cid = lax.broadcasted_iota(jnp.int32, (RP, 208), 1)
    pick = (cid == ((rid & 1) * ROWS + (rid >> 1)) * 8 + head) & (rid < STEPS * ROWS)
    tokens = jnp.dot(
        pick.astype(F32).astype(BF16),
        nkv[...].astype(F32).reshape(208, 2 * HD).astype(BF16),
        preferred_element_type=F32,
    )
    fresh[...] = tokens
    count = 0
    for r in range(ROWS):
        anc = anchor[r]
        loc = anc - base
        stay = (loc >= 0) & (loc < ROWS)
        home = anc // ROWS
        table[A_SRC + r] = jnp.where(stay, loc, home)
        table[A_STAY + r] = stay.astype(jnp.int32)
        table[A_POS + r] = count
        table[ARRIVED + count] = home
        count = count + jnp.where(stay, 0, 1)
        asked = q[r].astype(F32)
        build[r, 0:2] = asked[:, :HD]
        build[r, 2:4] = asked[:, HD:]
        build[r, 4:6] = tokens[2 * r : 2 * r + 2, :HD]
        build[r, 6:8] = tokens[2 * r : 2 * r + 2, HD:]
        length = lens[r]
        build[r, 8:9] = jnp.full((1, HD), (length >> 7) * PAGE, jnp.int32).astype(F32)
        build[r, 9:10] = jnp.full((1, HD), length & (PAGE - 1), jnp.int32).astype(F32)
        packet = build[r].astype(BF16)
        mine[r] = packet
        pack[home] = packet


def layer_kernel(
    table, kv, pack, mine, w, res, gain,
    moved, upd, nrm,
    kvv, wv, res_win, res32, sbuf, recv, comp, rest_out, rest_in, rest_kept, pkt, qs, nks, nvs, lens, score,
    part, land1, half1, half2, land2, relay, back, back_out, back_in, hid, sq_own, sq_all,
    load_sem, keep_sem, swap_send, swap_recv, rest_send, rest_recv, page_send, page_recv, pkt_send, pkt_recv, back_send, back_recv,
    rs_send, rs_recv, sq_send, sq_recv,
):
    g = lax.axis_index("group")
    t = lax.axis_index("tp")
    parity = lax.rem(t, 2)
    get_kv = pltpu.make_async_copy(kv, kvv, load_sem.at[0])
    get_w = pltpu.make_async_copy(w, wv, load_sem.at[1])
    get_res = pltpu.make_async_copy(
        res.at[:, :, pl.ds(pl.multiple_of((t // 2) * 640, 128), 640)], res_win, load_sem.at[2]
    )
    get_kv.start()
    get_w.start()
    get_res.start()

    zs = [lax.rem(t + o, NT) for o in range(NT)]

    def at_z(o):
        return zs[o % NT]

    core, x, y = lax.rem(g, 2), lax.rem(g // 2, 4), g // 8
    ys = [lax.rem(y + k, 4) * 8 for k in range(4)]
    xs = [lax.rem(x + k, 4) * 2 for k in range(4)]
    cs = [core, 1 - core]
    ys_to = [ys[k] + core * (ys[-k % 4] - ys[k]) for k in range(4)]
    xs_to = [xs[k] + core * (xs[-k % 4] - xs[k]) for k in range(4)]
    offsets = torus_offsets()
    peers = [ys_to[ky] + xs_to[kx] + cs[kc] for _, ky, kx, kc in offsets]

    barrier = pltpu.get_barrier_semaphore()
    for d in peers:
        pl.semaphore_signal(barrier, inc=1, device_id=(d, t), device_id_type=MESH)
    for o in range(1, NT):
        pl.semaphore_signal(barrier, inc=1, device_id=(g, zs[o]), device_id_type=MESH)
    pl.semaphore_wait(barrier, NG + NT - 2)

    def group_copy(src, dst, send_sem, recv_sem, d):
        return pltpu.make_async_remote_copy(
            src_ref=src, dst_ref=dst, send_sem=send_sem, recv_sem=recv_sem,
            device_id=(d, t), device_id_type=MESH,
        )

    def all_copies(src, dst, send_sem, recv_sem):
        most = pl.ds(0, NG - 1)
        return group_copy(src.at[most], dst.at[most], send_sem, recv_sem, peers[0])

    for d in peers:
        group_copy(pack.at[d], pkt.at[g], pkt_send, pkt_recv, d).start()
    packets = all_copies(pack, pkt, pkt_send, pkt_recv)
    get_kv.wait()

    half = pl.ds(pl.multiple_of(parity * HALF, 16), HALF)

    def send_pages(first, last):
        for n in range(first, last):
            d = peers[n]
            sbuf[n] = kvv[table[SLOT_TO + d], half, :]
            group_copy(sbuf.at[n], recv.at[g], page_send, page_recv, d).start()

    def send_rests(first, last):
        for n in range(first, last):
            d = peers[n]
            rest_out[n] = kvv[table[SLOT_TO + d], 2 * HALF :, :]
            group_copy(rest_out.at[n], rest_in.at[g], rest_send, rest_recv, d).start()

    send_pages(0, 4)

    get_res.wait()
    res32[...] = jnp.zeros_like(res32)
    for a in range(ROWS):
        res32[2 * a : 2 * a + 2, :] = res_win[a].astype(F32)
    qs[...] = jnp.zeros_like(qs)
    nks[...] = jnp.zeros_like(nks)
    nvs[...] = jnp.zeros_like(nvs)
    lens[...] = jnp.zeros_like(lens)
    packets.wait_recv()
    send_pages(4, 8)

    for i in range(ROWS):
        at = table[B_SRC + i]
        stay = table[B_STAY + i]
        near = mine[at * stay].astype(F32)
        far = pkt[at * (1 - stay)].astype(F32)
        row = jnp.where(stay == 1, near, far)
        qs[2 * i : 2 * i + 2, :] = row[0:2]
        qs[RP + 2 * i : RP + 2 * i + 2, :] = row[2:4]
        nks[2 * i : 2 * i + 2, :] = row[4:6]
        nvs[2 * i : 2 * i + 2, :] = row[6:8]
        length = jnp.broadcast_to(row[8:9] + row[9:10], (2, HD))
        lens[2 * i : 2 * i + 2, :] = length
        lens[RP + 2 * i : RP + 2 * i + 2, :] = length

    qa = qs[...].astype(BF16)
    row_all = lax.broadcasted_iota(jnp.int32, (2 * RP, PAGE), 0) & (RP - 1)
    lane = lax.broadcasted_iota(jnp.int32, (2 * RP, PAGE), 1)
    row_b = row_all >> 1
    lane_f = lane.astype(F32)
    row_len = lens[...]
    sc = lax.dot_general(
        qa, nks[...].astype(BF16), (((1,), (1,)), ((), ())), preferred_element_type=F32
    ) * (HD**-0.5)
    sc = jnp.where(((lane >> 1) == row_b) & ((lane & 1) <= (row_all & 1)), sc, -1e30)
    score[SLOTS] = sc
    top = sc
    for c in range(SLOTS):
        sc = lax.dot_general(
            qa, kvv[c, :, :HD], (((1,), (1,)), ((), ())), preferred_element_type=F32
        ) * (HD**-0.5)
        pos = lane_f + (table[NUM + c] * PAGE).astype(F32)
        sc = jnp.where((row_b == table[OWN + c]) & (pos < row_len), sc, -1e30)
        score[c] = sc
        top = jnp.maximum(top, sc)
    send_pages(8, 12)
    top = jnp.max(top, axis=1, keepdims=True)
    weight = jnp.exp(score[SLOTS] - top)
    total = weight
    mixed = jnp.dot(weight.astype(BF16), nvs[...].astype(BF16), preferred_element_type=F32)
    for c in range(SLOTS):
        weight = jnp.exp(score[c] - top)
        total = total + weight
        mixed = mixed + jnp.dot(
            weight.astype(BF16), kvv[c, :, HD:], preferred_element_type=F32
        )
    mixed = mixed / jnp.sum(total, axis=1, keepdims=True)
    att = jnp.concatenate([mixed[:RP], mixed[RP:]], axis=1).astype(BF16)

    get_w.wait()
    low = lax.broadcasted_iota(jnp.int32, (16, 128), 1) < 64

    def project(m):
        pair = lax.rem(t // 2 + m, NT // 2)
        columns = pl.ds(pl.multiple_of(pair * 640, 128), 640)
        out = jnp.dot(att, wv[:, columns], preferred_element_type=F32)
        mid = out[:, 256:384]
        left, right = 2 * pair, 2 * pair + 1
        part[left, 0:32] = out[:, 0:128].astype(BF16)
        part[left, 32:64] = out[:, 128:256].astype(BF16)
        part[left, 64:80] = jnp.where(low, mid[:16], pltpu.roll(mid[16:], 64, 1)).astype(BF16)
        part[right, 0:32] = out[:, 384:512].astype(BF16)
        part[right, 32:64] = out[:, 512:640].astype(BF16)
        part[right, 64:80] = jnp.where(low, pltpu.roll(mid[:16], 64, 1), mid[16:]).astype(BF16)

    def z_copy(n, src, dst, o):
        return pltpu.make_async_remote_copy(
            src_ref=src, dst_ref=dst, send_sem=rs_send.at[n], recv_sem=rs_recv.at[n],
            device_id=(g, at_z(o)), device_id_type=MESH,
        )

    first = {
        1: z_copy(1, part.at[at_z(-7)], land1.at[1], -2),
        5: z_copy(5, part.at[at_z(7)], land1.at[5], 2),
        8: z_copy(8, part.at[at_z(8), pl.ds(0, 48)], half1, -3),
        9: z_copy(9, part.at[at_z(8), pl.ds(48, 32)], half2, 3),
        0: z_copy(0, part.at[at_z(-6)], land1.at[0], -1),
        4: z_copy(4, part.at[at_z(6)], land1.at[4], 1),
        3: z_copy(3, part.at[at_z(-4)], land1.at[3], -2),
        7: z_copy(7, part.at[at_z(4)], land1.at[7], 2),
        2: z_copy(2, part.at[at_z(-3)], land1.at[2], -1),
        6: z_copy(6, part.at[at_z(3)], land1.at[6], 1),
        10: z_copy(10, part.at[at_z(-1)], land2.at[0], -1),
        11: z_copy(11, part.at[at_z(1)], land2.at[1], 1),
    }
    for pairs, ready in (((4, 3, 5), (1, 5, 8, 9, 0, 4)), ((2, 6, 1, 7), (3, 7, 2, 6)), ((0,), (10, 11))):
        for m in pairs:
            project(m)
        for n in ready:
            first[n].start()
    send_pages(12, 22)
    second = [
        z_copy(12, relay.at[0], land2.at[2], -5),
        z_copy(13, relay.at[1], land2.at[3], 5),
        z_copy(14, relay.at[2], land2.at[4], -2),
        z_copy(15, relay.at[3], land2.at[5], 2),
    ]
    for n, o, a, b, c in ((0, -5, 0, 1, 8), (1, 5, 4, 5, 9)):
        first[a].wait_recv()
        first[b].wait_recv()
        first[c].wait_recv()
        whole = part[at_z(o)].astype(F32) + land1[a].astype(F32) + land1[b].astype(F32)
        if n == 0:
            relay[n, 0:48] = (whole[0:48] + half1[...].astype(F32)).astype(BF16)
            relay[n, 48:80] = whole[48:80].astype(BF16)
        else:
            relay[n, 0:48] = whole[0:48].astype(BF16)
            relay[n, 48:80] = (whole[48:80] + half2[...].astype(F32)).astype(BF16)
        second[n].start()
    for n, o, a, b in ((2, -2, 2, 3), (3, 2, 6, 7)):
        first[a].wait_recv()
        first[b].wait_recv()
        relay[n] = (
            part[at_z(o)].astype(F32) + land1[a].astype(F32) + land1[b].astype(F32)
        ).astype(BF16)
        second[n].start()
    send_pages(22, 31)
    acc = part[t].astype(F32)
    first[10].wait_recv()
    first[11].wait_recv()
    acc = acc + land2[0].astype(F32) + land2[1].astype(F32)
    for n in (2, 3):
        second[n].wait_recv()
        acc = acc + land2[2 + n].astype(F32)

    for n in (0, 1):
        second[n].wait_recv()
        acc = acc + land2[2 + n].astype(F32)

    back[...] = jnp.zeros_like(back)
    tail = jnp.concatenate([acc[64:80], pltpu.roll(acc[64:80], 64, 1)], axis=0)
    for i in range(ROWS):
        back[i, 0:2] = acc[2 * i : 2 * i + 2]
        back[i, 2:4] = acc[32 + 2 * i : 34 + 2 * i]
        back[i, 4:6] = tail[2 * i : 2 * i + 2]

    for d in peers:
        back_out[d] = back[table[RET_SRC + d]]
        group_copy(back_out.at[d], back_in.at[g], back_send, back_recv, d).start()
    returns = all_copies(back_out, back_in, back_send, back_recv)
    pages = all_copies(sbuf, recv, page_send, page_recv)
    pages.wait_recv()
    for j in range(MOVED):
        comp[j] = recv[table[ARRIVED + j]]

    def swap_copy(n, first, count):
        some = pl.ds(first, count)
        return pltpu.make_async_remote_copy(
            src_ref=comp.at[some], dst_ref=moved.at[some, half],
            send_sem=swap_send.at[n], recv_sem=swap_recv.at[n],
            device_id=(g, t + 1 - 2 * parity), device_id_type=MESH,
        )

    swaps = [swap_copy(0, 0, 6), swap_copy(1, 6, MOVED - 6)]
    swaps[0].start()
    keep = pltpu.make_async_copy(comp, moved.at[:, half], keep_sem.at[0])
    keep.start()
    send_rests(0, 16)

    hid[...] = jnp.zeros_like(hid)
    returns.wait_recv()
    for r in range(ROWS):
        at = table[A_SRC + r]
        stay = table[A_STAY + r]
        row = jnp.where(stay == 1, back[at * stay], back_in[at * (1 - stay)])
        for j in range(3):
            hid[j, 2 * r : 2 * r + 2, :] = row[2 * j : 2 * j + 2]

    even = parity == 0
    mid = res32[:, 256:384]
    sum_a = hid[0] + jnp.where(even, res32[:, 0:128], res32[:, 384:512])
    sum_b = hid[1] + jnp.where(even, res32[:, 128:256], res32[:, 512:640])
    sum_h = hid[2] + jnp.where(even, mid, pltpu.roll(mid, 64, 1))
    own = lax.broadcasted_iota(jnp.int32, (RP, 128), 1) < 64
    sum_h = jnp.where(own, sum_h, 0.0)
    square = jnp.sum(sum_a * sum_a + sum_b * sum_b + sum_h * sum_h, axis=1, keepdims=True)
    diag = lax.broadcasted_iota(jnp.int32, (RP, 128), 0) == lax.broadcasted_iota(
        jnp.int32, (RP, 128), 1
    )
    sq_own[...] = jnp.sum(jnp.where(diag, square, 0.0), axis=0, keepdims=True)

    for o in (8, 7, 9, 6, 10, 5, 11, 4, 12, 3, 13, 2, 14, 1, 15):
        pltpu.make_async_remote_copy(
            src_ref=sq_own, dst_ref=sq_all.at[o], send_sem=sq_send, recv_sem=sq_recv,
            device_id=(g, zs[o]), device_id_type=MESH,
        ).start()
    swaps[1].start()
    send_rests(16, 31)
    most = pl.ds(1, NT - 1)
    squares = pltpu.make_async_remote_copy(
        src_ref=sq_all.at[most], dst_ref=sq_all.at[most], send_sem=sq_send, recv_sem=sq_recv,
        device_id=(g, zs[1]), device_id_type=MESH,
    )
    tail = sum_h[:, 0:64]
    value = jnp.where(
        even,
        jnp.concatenate([sum_a, sum_b, tail], axis=1),
        jnp.concatenate([tail, sum_a, sum_b], axis=1),
    )
    for a in range(ROWS):
        upd[a] = value[2 * a : 2 * a + 2, :].astype(BF16)
    scaled = value * gain[...].astype(F32).reshape(1, COLS)
    whole = sq_own[...]
    squares.wait_recv()
    for k in range(1, NT):
        whole = whole + sq_all[k]
    inverse = lax.rsqrt(whole * (1.0 / D) + 1e-6)
    factor = jnp.sum(jnp.where(diag, inverse, 0.0), axis=1, keepdims=True)
    scaled = scaled * factor
    for a in range(ROWS):
        nrm[a] = scaled[2 * a : 2 * a + 2, :].astype(BF16)

    for copy in first.values():
        copy.wait_send()
    for copy in second:
        copy.wait_send()
    packets.wait_send()
    returns.wait_send()
    squares.wait_send()
    rests = all_copies(rest_out, rest_in, rest_send, rest_recv)
    rests.wait_recv()
    for j in range(MOVED):
        rest_kept[j] = rest_in[table[ARRIVED + j]]
    keep_rest = pltpu.make_async_copy(rest_kept, moved.at[:, pl.ds(2 * HALF, REST)], keep_sem.at[1])
    keep_rest.start()
    pages.wait_send()
    rests.wait_send()
    keep.wait()
    keep_rest.wait()
    for copy in swaps:
        copy.wait()


def place_kernel(
    table, lens, pb, pa, kv, moved, fresh, upd_in, nrm_in, kva, upd, nrm, buf, page_sem, out_sem
):
    passed = [
        pltpu.make_async_copy(upd_in, upd, out_sem.at[1]),
        pltpu.make_async_copy(nrm_in, nrm, out_sem.at[2]),
    ]
    for copy in passed:
        copy.start()

    def fetch(r, carry):
        need = (lens[r] + (STEPS + PAGE - 1)) >> 7
        at = table[A_SRC + r]
        pos = table[A_POS + r]
        stay = table[A_STAY + r]
        for j in range(4):
            @pl.when((j < need) & (stay == 0))
            def _():
                c = pa[j, r]
                pltpu.make_async_copy(moved.at[pos], buf.at[c], page_sem.at[c]).start()

            @pl.when((j < need) & (stay == 1))
            def _():
                c = pa[j, r]
                pltpu.make_async_copy(kv.at[pb[j, at]], buf.at[c], page_sem.at[c]).start()
        return carry

    lax.fori_loop(0, ROWS, fetch, 0)
    lane_row = lax.broadcasted_iota(jnp.int32, (16, 2 * HD), 0)
    for c in range(SLOTS):
        pltpu.make_async_copy(kv.at[0], buf.at[c], page_sem.at[c]).wait()

    def write(r, carry):
        for s in range(STEPS):
            p = lens[r] + s
            c = pa[p >> 7, r]
            e = p & (PAGE - 1)
            base = pl.multiple_of((e >> 4) << 4, 16)
            block = buf[c, pl.ds(base, 16), :].astype(F32)
            token = fresh[pl.ds(2 * r + s, 1), :]
            buf[c, pl.ds(base, 16), :] = jnp.where(
                lane_row == (e & 15), token, block
            ).astype(BF16)
        return carry

    lax.fori_loop(0, ROWS, write, 0)
    out = pltpu.make_async_copy(buf, kva, out_sem.at[0])
    out.start()
    for copy in passed:
        copy.wait()
    out.wait()


VM = pl.BlockSpec(memory_space=pltpu.VMEM)
SM = pl.BlockSpec(memory_space=pltpu.SMEM)
HBM = pl.BlockSpec(memory_space=pltpu.HBM)
DMA = pltpu.SemaphoreType.DMA


def on_device(
    lengths, destination, page_before, page_after, kv_cache,
    queries, new_kv, residual, out_weight, norm_gain,
):
    kv = kv_cache[0, 0]
    pb, pa = page_before.T, page_after.T
    table, pack, mine, fresh = pl.pallas_call(
        route_kernel,
        out_shape=(
            jax.ShapeDtypeStruct((TABLE,), jnp.int32),
            jax.ShapeDtypeStruct((NG, 16, 128), BF16),
            jax.ShapeDtypeStruct((16, 16, 128), BF16),
            jax.ShapeDtypeStruct((RP, 2 * HD), F32),
        ),
        in_specs=[HBM] * 5,
        out_specs=(SM, VM, VM, VM),
        scratch_shapes=[
            pltpu.SMEM((ROWS,), jnp.int32),
            pltpu.SMEM((NG * ROWS,), jnp.int32),
            pltpu.SMEM((4, ROWS), jnp.int32),
            pltpu.VMEM((ROWS, STEPS, 2 * HD), BF16),
            pltpu.VMEM((STEPS, ROWS, 8, 2 * HD), BF16),
            pltpu.SMEM((ROWS + 1,), jnp.int32),
            pltpu.VMEM((ROWS, 16, 128), F32),
            DMA((5,)),
        ],
        compiler_params=pltpu.CompilerParams(vmem_limit_bytes=60 << 20),
        name="route",
    )(lengths, destination, pb, queries.transpose(1, 0, 2), new_kv)
    moved, upd, nrm = pl.pallas_call(
        layer_kernel,
        out_shape=(
            jax.ShapeDtypeStruct((MOVED, PAGE, 2 * HD), BF16),
            jax.ShapeDtypeStruct((ROWS, STEPS, COLS), BF16),
            jax.ShapeDtypeStruct((ROWS, STEPS, COLS), BF16),
        ),
        in_specs=[SM, HBM, HBM, VM, HBM, HBM, VM],
        out_specs=(HBM, VM, VM),
        scratch_shapes=[
            pltpu.VMEM((SLOTS, PAGE, 2 * HD), BF16),
            pltpu.VMEM((2 * HD, D), BF16),
            pltpu.VMEM((ROWS, STEPS, 640), BF16),
            pltpu.VMEM((RP, 640), F32),
            pltpu.VMEM((NG, HALF, 2 * HD), BF16),
            pltpu.VMEM((NG, HALF, 2 * HD), BF16),
            pltpu.VMEM((MOVED, HALF, 2 * HD), BF16),
            pltpu.VMEM((NG, REST, 2 * HD), BF16),
            pltpu.VMEM((NG, REST, 2 * HD), BF16),
            pltpu.VMEM((MOVED, REST, 2 * HD), BF16),
            pltpu.VMEM((NG, 16, 128), BF16),
            pltpu.VMEM((2 * RP, HD), F32),
            pltpu.VMEM((128, HD), F32),
            pltpu.VMEM((128, HD), F32),
            pltpu.VMEM((2 * RP, HD), F32),
            pltpu.VMEM((SLOTS + 1, 2 * RP, PAGE), F32),
            pltpu.VMEM((NT, BLK, 128), BF16),
            pltpu.VMEM((8, BLK, 128), BF16),
            pltpu.VMEM((48, 128), BF16),
            pltpu.VMEM((32, 128), BF16),
            pltpu.VMEM((6, BLK, 128), BF16),
            pltpu.VMEM((4, BLK, 128), BF16),
            pltpu.VMEM((16, 8, 128), F32),
            pltpu.VMEM((NG, 8, 128), F32),
            pltpu.VMEM((NG, 8, 128), F32),
            pltpu.VMEM((3, RP, 128), F32),
            pltpu.VMEM((1, 128), F32),
            pltpu.VMEM((NT, 1, 128), F32),
            DMA((3,)),
            DMA((2,)),
            DMA((2,)),
            DMA((2,)),
            DMA(()),
            DMA(()),
            DMA(()),
            DMA(()),
            DMA(()),
            DMA(()),
            DMA(()),
            DMA(()),
            DMA((16,)),
            DMA((16,)),
            DMA(()),
            DMA(()),
        ],
        compiler_params=pltpu.CompilerParams(
            collective_id=0, has_side_effects=True, vmem_limit_bytes=58 << 20
        ),
        name="layer",
    )(
        table, kv, pack, mine, out_weight, residual.transpose(1, 0, 2),
        norm_gain,
    )
    kva, upd, nrm = pl.pallas_call(
        place_kernel,
        out_shape=(
            jax.ShapeDtypeStruct((SLOTS, PAGE, 2 * HD), BF16),
            jax.ShapeDtypeStruct((ROWS, STEPS, COLS), BF16),
            jax.ShapeDtypeStruct((ROWS, STEPS, COLS), BF16),
        ),
        in_specs=[SM, SM, SM, SM, HBM, HBM, VM, HBM, HBM],
        out_specs=(HBM, HBM, HBM),
        scratch_shapes=[
            pltpu.VMEM((SLOTS, PAGE, 2 * HD), BF16),
            DMA((SLOTS,)),
            DMA((3,)),
        ],
        compiler_params=pltpu.CompilerParams(vmem_limit_bytes=60 << 20),
        name="place",
    )(table, lengths, pb, pa, kv, moved, fresh, upd, nrm)
    return kva[None, None], upd.transpose(1, 0, 2), nrm.transpose(1, 0, 2)


def solution(mesh):
    in_specs = (
        P("group"),
        P(),
        P("group", None),
        P("group", None),
        P("group", "tp", None, None, None),
        P(None, "group", "tp"),
        P(None, "group", None, None),
        P(None, "group", None),
        P("tp", None),
        P("tp"),
    )
    out_specs = (P("group", "tp", None, None, None), P(None, "group", "tp"), P(None, "group", "tp"))
    return jax.shard_map(
        on_device, mesh=mesh, in_specs=in_specs, out_specs=out_specs, check_vma=False
    )
```

```python
import jax
import jax.numpy as jnp
from jax import lax
from jax.experimental import pallas as pl
from jax.experimental.pallas import tpu as pltpu
from jax.sharding import PartitionSpec as P

MESH = pl.DeviceIdType.MESH
NG = 32
NT = 16
ROWS = 13
STEPS = 2
SLOTS = 16
PAGE = 128
HD = 128
RP = 32
D = 5120
COLS = D // NT
BLK = 80
F32 = jnp.float32
BF16 = jnp.bfloat16

A_SRC, A_STAY, A_POS = 0, 16, 32
TABLE = 48
MOVED = 11
HALF = PAGE // 2


def torus_offsets():
    found = []
    for ky in range(4):
        for kx in range(4):
            for kc in range(2):
                if (ky, kx, kc) != (0, 0, 0):
                    found.append((min(ky, 4 - ky) + min(kx, 4 - kx), ky, kx, kc))
    return sorted(found, key=lambda o: -o[0])


def layer_kernel(
    lens_in, dest_in, pb_in, q_in, nkv_in, kv, w, res, gain_in,
    table, moved, upd_out, nrm_out, fresh_out,
    length_of, dest, pb, dest_row, q, nkv, build, fresh, pack, slots,
    mine, gain, upd, nrm, kvv, wv, res_win, res32, sbuf, recv, comp, pkt, qs, nks, nvs, lens, pages_of, score,
    part, land1, half1, half2, land2, relay, back, back_out, back_in, hid, sq_own, sq_all,
    load_sem, keep_sem, swap_send, swap_recv, page_send, page_recv, pkt_send, pkt_recv, back_send, back_recv,
    rs_send, rs_recv, sq_send, sq_recv,
):
    g = lax.axis_index("group")
    t = lax.axis_index("tp")
    parity = lax.rem(t, 2)
    get_kv = pltpu.make_async_copy(kv, kvv, load_sem.at[0])
    get_w = pltpu.make_async_copy(w, wv, load_sem.at[1])
    get_res = pltpu.make_async_copy(
        res.at[:, :, pl.ds(pl.multiple_of((t // 2) * 640, 128), 640)], res_win, load_sem.at[2]
    )
    get_gain = pltpu.make_async_copy(gain_in, gain, load_sem.at[3])
    small = [
        pltpu.make_async_copy(src, dst, load_sem.at[4 + n])
        for n, (src, dst) in enumerate(
            (
                (dest_in, dest_row), (dest_in, dest), (lens_in, length_of), (pb_in, pb),
                (nkv_in, nkv), (q_in, q),
            )
        )
    ]
    for load in small:
        load.start()
    get_kv.start()
    get_gain.start()
    get_w.start()
    get_res.start()

    zs = [lax.rem(t + o, NT) for o in range(NT)]

    def at_z(o):
        return zs[o % NT]

    core, x, y = lax.rem(g, 2), lax.rem(g // 2, 4), g // 8
    ys = [lax.rem(y + k, 4) * 8 for k in range(4)]
    xs = [lax.rem(x + k, 4) * 2 for k in range(4)]
    cs = [core, 1 - core]
    ys_to = [ys[k] + core * (ys[-k % 4] - ys[k]) for k in range(4)]
    xs_to = [xs[k] + core * (xs[-k % 4] - xs[k]) for k in range(4)]
    offsets = torus_offsets()
    peers = [ys_to[ky] + xs_to[kx] + cs[kc] for _, ky, kx, kc in offsets]

    barrier = pltpu.get_barrier_semaphore()
    for d in peers:
        pl.semaphore_signal(barrier, inc=1, device_id=(d, t), device_id_type=MESH)
    for o in range(1, NT):
        pl.semaphore_signal(barrier, inc=1, device_id=(g, zs[o]), device_id_type=MESH)

    build[...] = jnp.zeros_like(build)
    for load in small:
        load.wait()
    base = g * ROWS
    dest_all = dest_row[...].reshape(1, NG * ROWS)
    lane = lax.broadcasted_iota(jnp.int32, (16, NG * ROWS), 1)
    row = lax.broadcasted_iota(jnp.int32, (16, NG * ROWS), 0)
    anchor = jnp.max(jnp.where(dest_all == base + row, lane, 0), axis=1, keepdims=True)
    peer_row = lax.broadcasted_iota(jnp.int32, (NG, 1), 0)
    peer_col = jnp.full((NG, 1), -1, jnp.int32)
    for n, d in enumerate(peers):
        peer_col = jnp.where(peer_row == n, d, peer_col)
    lane = lax.broadcasted_iota(jnp.int32, (NG, NG * ROWS), 1)
    taken = (lane >= base) & (lane < base + ROWS)
    taken = taken & (dest_all >= peer_col * ROWS) & (dest_all < peer_col * ROWS + ROWS)
    taker = jnp.max(jnp.where(taken, lane - base, 0), axis=1, keepdims=True)

    rid = lax.broadcasted_iota(jnp.int32, (RP, 208), 0)
    cid = lax.broadcasted_iota(jnp.int32, (RP, 208), 1)
    pick = (cid == ((rid & 1) * ROWS + (rid >> 1)) * 8 + t // 2) & (rid < STEPS * ROWS)
    tokens = jnp.dot(
        pick.astype(F32).astype(BF16),
        nkv[...].astype(F32).reshape(208, 2 * HD).astype(BF16),
        preferred_element_type=F32,
    )
    fresh[...] = tokens
    put_fresh = pltpu.make_async_copy(fresh, fresh_out, load_sem.at[10])
    put_fresh.start()
    lane = lax.broadcasted_iota(jnp.int32, (1, 128), 1)
    homes = jnp.full((1, 128), -2, jnp.int32)
    count = 0
    for r in range(ROWS):
        anc = anchor[r, 0]
        loc = anc - base
        stay = (loc >= 0) & (loc < ROWS)
        home = anc // ROWS
        homes = jnp.where(lane == r, home, homes)
        table[A_SRC + r] = jnp.where(stay, loc, home)
        table[A_STAY + r] = stay.astype(jnp.int32)
        table[A_POS + r] = count
        count = count + jnp.where(stay, 0, 1)
        asked = q[r].astype(F32)
        build[r, 0:2] = asked[:, :HD]
        build[r, 2:4] = asked[:, HD:]
        build[r, 4:6] = tokens[2 * r : 2 * r + 2, :HD]
        build[r, 6:8] = tokens[2 * r : 2 * r + 2, HD:]
        length = length_of[r]
        build[r, 8:9] = jnp.full((1, HD), (length >> 7) * PAGE, jnp.int32).astype(F32)
        build[r, 9:10] = jnp.full((1, HD), length & (PAGE - 1), jnp.int32).astype(F32)
        mine[r] = build[r].astype(BF16)
    giver = jnp.max(jnp.where(peer_col == homes, lane, 0), axis=1, keepdims=True)
    for n in range(NG - 1):
        pack[n] = mine[giver[n, 0]]
        slots[n] = taker[n, 0]
    pl.semaphore_wait(barrier, NG + NT - 2)

    def group_copy(src, dst, send_sem, recv_sem, d):
        return pltpu.make_async_remote_copy(
            src_ref=src, dst_ref=dst, send_sem=send_sem, recv_sem=recv_sem,
            device_id=(d, t), device_id_type=MESH,
        )

    def all_copies(src, dst, send_sem, recv_sem):
        most = pl.ds(0, NG - 1)
        return group_copy(src.at[most], dst.at[most], send_sem, recv_sem, peers[0])

    for n, d in enumerate(peers):
        group_copy(pack.at[n], pkt.at[g], pkt_send, pkt_recv, d).start()
    packets = all_copies(pack, pkt, pkt_send, pkt_recv)
    get_kv.wait()

    half = pl.ds(pl.multiple_of(parity * HALF, HALF), HALF)

    def send_pages(first, last):
        for n in range(first, last):
            d = peers[n]
            sbuf[n] = kvv[pb[0, slots[n]], half, :]
            group_copy(sbuf.at[n], recv.at[g], page_send, page_recv, d).start()

    send_pages(0, 4)

    get_res.wait()
    res32[...] = jnp.zeros_like(res32)
    for a in range(ROWS):
        res32[2 * a : 2 * a + 2, :] = res_win[a].astype(F32)
    qs[...] = jnp.zeros_like(qs)
    nks[...] = jnp.zeros_like(nks)
    nvs[...] = jnp.zeros_like(nvs)
    lens[...] = jnp.zeros_like(lens)
    pages_of[...] = jnp.full_like(pages_of, -1)
    get_gain.wait()
    packets.wait_recv()
    send_pages(4, 8)

    for i in range(ROWS):
        to = dest[base + i]
        loc = to - base
        stay = ((loc >= 0) & (loc < ROWS)).astype(jnp.int32)
        near = mine[loc * stay].astype(F32)
        far = pkt[(to // ROWS) * (1 - stay)].astype(F32)
        got = jnp.where(stay == 1, near, far)
        qs[2 * i : 2 * i + 2, :] = got[0:2]
        qs[RP + 2 * i : RP + 2 * i + 2, :] = got[2:4]
        nks[2 * i : 2 * i + 2, :] = got[4:6]
        nvs[2 * i : 2 * i + 2, :] = got[6:8]
        lens[2 * i : 2 * i + 2, :] = jnp.broadcast_to(got[8:9] + got[9:10], (2, HD))
        need = 1 + stay * (((length_of[loc * stay] + (STEPS + PAGE - 1)) >> 7) - 1)
        for j in range(4):
            page = jnp.where(j < need, pb[j, i], -1)
            pages_of[j, 2 * i : 2 * i + 2, :] = jnp.full((2, HD), page, jnp.int32)

    qa = qs[...].astype(BF16)
    row_all = lax.broadcasted_iota(jnp.int32, (2 * RP, PAGE), 0) & (RP - 1)
    lane = lax.broadcasted_iota(jnp.int32, (2 * RP, PAGE), 1)
    row_b = row_all >> 1
    lane_f = lane.astype(F32)
    row_len = jnp.concatenate([lens[...], lens[...]], axis=0)
    row_page = [jnp.concatenate([pages_of[j], pages_of[j]], axis=0) for j in range(4)]
    sc = lax.dot_general(
        qa, nks[...].astype(BF16), (((1,), (1,)), ((), ())), preferred_element_type=F32
    ) * (HD**-0.5)
    sc = jnp.where(((lane >> 1) == row_b) & ((lane & 1) <= (row_all & 1)), sc, -1e30)
    score[SLOTS] = sc
    top = sc
    for c in range(SLOTS):
        sc = lax.dot_general(
            qa, kvv[c, :, :HD], (((1,), (1,)), ((), ())), preferred_element_type=F32
        ) * (HD**-0.5)
        held = jnp.zeros_like(row_len)
        for j in range(4):
            held = jnp.where(row_page[j] == c, row_len - j * PAGE, held)
        sc = jnp.where(lane_f < held, sc, -1e30)
        score[c] = sc
        top = jnp.maximum(top, sc)
    send_pages(8, 13)
    top = jnp.max(top, axis=1, keepdims=True)
    weight = jnp.exp(score[SLOTS] - top)
    total = weight
    mixed = jnp.dot(weight.astype(BF16), nvs[...].astype(BF16), preferred_element_type=F32)
    for c in range(SLOTS):
        weight = jnp.exp(score[c] - top)
        total = total + weight
        mixed = mixed + jnp.dot(
            weight.astype(BF16), kvv[c, :, HD:], preferred_element_type=F32
        )
    mixed = mixed / jnp.sum(total, axis=1, keepdims=True)
    att = jnp.concatenate([mixed[:RP], mixed[RP:]], axis=1).astype(BF16)

    get_w.wait()
    send_pages(13, 17)
    low = lax.broadcasted_iota(jnp.int32, (16, 128), 1) < 64

    def project(m):
        pair = lax.rem(t // 2 + m, NT // 2)
        columns = pl.ds(pl.multiple_of(pair * 640, 128), 640)
        out = jnp.dot(att, wv[:, columns], preferred_element_type=F32)
        mid = out[:, 256:384]
        left, right = 2 * pair, 2 * pair + 1
        part[left, 0:32] = out[:, 0:128].astype(BF16)
        part[left, 32:64] = out[:, 128:256].astype(BF16)
        part[left, 64:80] = jnp.where(low, mid[:16], pltpu.roll(mid[16:], 64, 1)).astype(BF16)
        part[right, 0:32] = out[:, 384:512].astype(BF16)
        part[right, 32:64] = out[:, 512:640].astype(BF16)
        part[right, 64:80] = jnp.where(low, pltpu.roll(mid[:16], 64, 1), mid[16:]).astype(BF16)

    def z_copy(n, src, dst, o):
        return pltpu.make_async_remote_copy(
            src_ref=src, dst_ref=dst, send_sem=rs_send.at[n], recv_sem=rs_recv.at[n],
            device_id=(g, at_z(o)), device_id_type=MESH,
        )

    first = {
        1: z_copy(1, part.at[at_z(-7)], land1.at[1], -2),
        5: z_copy(5, part.at[at_z(7)], land1.at[5], 2),
        8: z_copy(8, part.at[at_z(8), pl.ds(0, 48)], half1, -3),
        9: z_copy(9, part.at[at_z(8), pl.ds(48, 32)], half2, 3),
        0: z_copy(0, part.at[at_z(-6)], land1.at[0], -1),
        4: z_copy(4, part.at[at_z(6)], land1.at[4], 1),
        3: z_copy(3, part.at[at_z(-4)], land1.at[3], -2),
        7: z_copy(7, part.at[at_z(4)], land1.at[7], 2),
        2: z_copy(2, part.at[at_z(-3)], land1.at[2], -1),
        6: z_copy(6, part.at[at_z(3)], land1.at[6], 1),
        10: z_copy(10, part.at[at_z(-1)], land2.at[0], -1),
        11: z_copy(11, part.at[at_z(1)], land2.at[1], 1),
    }
    for pairs, ready in (((4, 3, 5), (1, 5, 8, 9, 0, 4)), ((2, 6, 1, 7), (3, 7, 2, 6)), ((0,), (10, 11))):
        for m in pairs:
            project(m)
        for n in ready:
            first[n].start()
    send_pages(17, 24)
    second = [
        z_copy(12, relay.at[0], land2.at[2], -5),
        z_copy(13, relay.at[1], land2.at[3], 5),
        z_copy(14, relay.at[2], land2.at[4], -2),
        z_copy(15, relay.at[3], land2.at[5], 2),
    ]
    for n, o, a, b, c in ((0, -5, 0, 1, 8), (1, 5, 4, 5, 9)):
        first[a].wait_recv()
        first[b].wait_recv()
        first[c].wait_recv()
        whole = part[at_z(o)].astype(F32) + land1[a].astype(F32) + land1[b].astype(F32)
        if n == 0:
            relay[n, 0:48] = (whole[0:48] + half1[...].astype(F32)).astype(BF16)
            relay[n, 48:80] = whole[48:80].astype(BF16)
        else:
            relay[n, 0:48] = whole[0:48].astype(BF16)
            relay[n, 48:80] = (whole[48:80] + half2[...].astype(F32)).astype(BF16)
        second[n].start()
    for n, o, a, b in ((2, -2, 2, 3), (3, 2, 6, 7)):
        first[a].wait_recv()
        first[b].wait_recv()
        relay[n] = (
            part[at_z(o)].astype(F32) + land1[a].astype(F32) + land1[b].astype(F32)
        ).astype(BF16)
        second[n].start()
    send_pages(24, 31)
    acc = part[t].astype(F32)
    first[10].wait_recv()
    first[11].wait_recv()
    acc = acc + land2[0].astype(F32) + land2[1].astype(F32)
    for n in (2, 3):
        second[n].wait_recv()
        acc = acc + land2[2 + n].astype(F32)

    pages = all_copies(sbuf, recv, page_send, page_recv)
    pages.wait_recv()
    for j in range(MOVED):
        source = 0
        for r in range(ROWS):
            counts = (1 - table[A_STAY + r]) * (table[A_POS + r] == j).astype(jnp.int32)
            source = source + counts * table[A_SRC + r]
        comp[j] = recv[source]

    def swap_copy(n, first, count):
        some = pl.ds(first, count)
        return pltpu.make_async_remote_copy(
            src_ref=comp.at[some], dst_ref=moved.at[some, half],
            send_sem=swap_send.at[n], recv_sem=swap_recv.at[n],
            device_id=(g, t + 1 - 2 * parity), device_id_type=MESH,
        )

    swaps = [swap_copy(0, 0, 3), swap_copy(1, 3, 4), swap_copy(2, 7, 4)]
    swaps[0].start()
    keep = pltpu.make_async_copy(comp, moved.at[:, half], keep_sem)
    keep.start()
    for n in (0, 1):
        second[n].wait_recv()
        acc = acc + land2[2 + n].astype(F32)

    back[...] = jnp.zeros_like(back)
    tail = jnp.concatenate([acc[64:80], pltpu.roll(acc[64:80], 64, 1)], axis=0)
    for i in range(ROWS):
        back[i, 0:2] = acc[2 * i : 2 * i + 2]
        back[i, 2:4] = acc[32 + 2 * i : 34 + 2 * i]
        back[i, 4:6] = tail[2 * i : 2 * i + 2]

    for n, d in enumerate(peers):
        back_out[n] = back[slots[n]]
        group_copy(back_out.at[n], back_in.at[g], back_send, back_recv, d).start()
    returns = all_copies(back_out, back_in, back_send, back_recv)
    swaps[1].start()

    hid[...] = jnp.zeros_like(hid)
    returns.wait_recv()
    for r in range(ROWS):
        at = table[A_SRC + r]
        stay = table[A_STAY + r]
        row = jnp.where(stay == 1, back[at * stay], back_in[at * (1 - stay)])
        for j in range(3):
            hid[j, 2 * r : 2 * r + 2, :] = row[2 * j : 2 * j + 2]

    even = parity == 0
    mid = res32[:, 256:384]
    sum_a = hid[0] + jnp.where(even, res32[:, 0:128], res32[:, 384:512])
    sum_b = hid[1] + jnp.where(even, res32[:, 128:256], res32[:, 512:640])
    sum_h = hid[2] + jnp.where(even, mid, pltpu.roll(mid, 64, 1))
    own = lax.broadcasted_iota(jnp.int32, (RP, 128), 1) < 64
    sum_h = jnp.where(own, sum_h, 0.0)
    square = jnp.sum(sum_a * sum_a + sum_b * sum_b + sum_h * sum_h, axis=1, keepdims=True)
    diag = lax.broadcasted_iota(jnp.int32, (RP, 128), 0) == lax.broadcasted_iota(
        jnp.int32, (RP, 128), 1
    )
    sq_own[...] = jnp.sum(jnp.where(diag, square, 0.0), axis=0, keepdims=True)

    for o in (8, 7, 9, 6, 10, 5, 11, 4, 12, 3, 13, 2, 14, 1, 15):
        pltpu.make_async_remote_copy(
            src_ref=sq_own, dst_ref=sq_all.at[o], send_sem=sq_send, recv_sem=sq_recv,
            device_id=(g, zs[o]), device_id_type=MESH,
        ).start()
    swaps[2].start()
    most = pl.ds(1, NT - 1)
    squares = pltpu.make_async_remote_copy(
        src_ref=sq_all.at[most], dst_ref=sq_all.at[most], send_sem=sq_send, recv_sem=sq_recv,
        device_id=(g, zs[1]), device_id_type=MESH,
    )
    tail = sum_h[:, 0:64]
    value = jnp.where(
        even,
        jnp.concatenate([sum_a, sum_b, tail], axis=1),
        jnp.concatenate([tail, sum_a, sum_b], axis=1),
    )
    for a in range(ROWS):
        upd[a] = value[2 * a : 2 * a + 2, :].astype(BF16)
    put_upd = pltpu.make_async_copy(upd, upd_out, load_sem.at[0])
    put_upd.start()
    scaled = value * gain[...].astype(F32).reshape(1, COLS)
    whole = sq_own[...]
    squares.wait_recv()
    for k in range(1, NT):
        whole = whole + sq_all[k]
    inverse = lax.rsqrt(whole * (1.0 / D) + 1e-6)
    factor = jnp.sum(jnp.where(diag, inverse, 0.0), axis=1, keepdims=True)
    scaled = scaled * factor
    for a in range(ROWS):
        nrm[a] = scaled[2 * a : 2 * a + 2, :].astype(BF16)
    put_nrm = pltpu.make_async_copy(nrm, nrm_out, load_sem.at[1])
    put_nrm.start()

    for copy in first.values():
        copy.wait_send()
    for copy in second:
        copy.wait_send()
    packets.wait_send()
    returns.wait_send()
    squares.wait_send()
    pages.wait_send()
    keep.wait()
    for copy in swaps:
        copy.wait()
    put_fresh.wait()
    put_upd.wait()
    put_nrm.wait()


def place_kernel(
    table, lens, pb, pa, kv, moved, fresh, upd_in, nrm_in, kva, upd, nrm, buf, page_sem, out_sem
):
    passed = [
        pltpu.make_async_copy(upd_in, upd, out_sem.at[1]),
        pltpu.make_async_copy(nrm_in, nrm, out_sem.at[2]),
    ]
    for copy in passed:
        copy.start()

    def fetch(r, carry):
        need = (lens[r] + (STEPS + PAGE - 1)) >> 7
        at = table[A_SRC + r]
        stay = table[A_STAY + r]

        @pl.when(stay == 0)
        def _():
            c = pa[0, r]
            pltpu.make_async_copy(moved.at[table[A_POS + r]], buf.at[c], page_sem.at[c]).start()

        @pl.when(stay == 1)
        def _():
            def page(j, carry):
                c = pa[j, r]
                pltpu.make_async_copy(kv.at[pb[j, at]], buf.at[c], page_sem.at[c]).start()
                return carry

            lax.fori_loop(0, need, page, 0)

        return carry

    lax.fori_loop(0, ROWS, fetch, 0)
    lane_row = lax.broadcasted_iota(jnp.int32, (16, 2 * HD), 0)
    for c in range(SLOTS):
        pltpu.make_async_copy(kv.at[0], buf.at[c], page_sem.at[c]).wait()

    def patch(r, s, p, both):
        c = pa[p >> 7, r]
        e = p & (PAGE - 1)
        base = pl.multiple_of((e >> 4) << 4, 16)
        block = buf[c, pl.ds(base, 16), :].astype(F32)
        block = jnp.where(lane_row == (e & 15), fresh[pl.ds(2 * r + s, 1), :], block)
        if both:
            block = jnp.where(lane_row == (e & 15) + 1, fresh[pl.ds(2 * r + 1, 1), :], block)
        buf[c, pl.ds(base, 16), :] = block.astype(BF16)

    def write(r, carry):
        p = lens[r]
        patch(r, 0, p, True)

        @pl.when((p & 15) == 15)
        def _():
            patch(r, 1, p + 1, False)

        return carry

    lax.fori_loop(0, ROWS, write, 0)
    out = pltpu.make_async_copy(buf, kva, out_sem.at[0])
    out.start()
    for copy in passed:
        copy.wait()
    out.wait()


VM = pl.BlockSpec(memory_space=pltpu.VMEM)
SM = pl.BlockSpec(memory_space=pltpu.SMEM)
HBM = pl.BlockSpec(memory_space=pltpu.HBM)
DMA = pltpu.SemaphoreType.DMA


def on_device(
    lengths, destination, page_before, page_after, kv_cache,
    queries, new_kv, residual, out_weight, norm_gain,
):
    kv = kv_cache[0, 0]
    pb, pa = page_before.T, page_after.T
    table, moved, upd, nrm, fresh = pl.pallas_call(
        layer_kernel,
        out_shape=(
            jax.ShapeDtypeStruct((TABLE,), jnp.int32),
            jax.ShapeDtypeStruct((MOVED, PAGE, 2 * HD), BF16),
            jax.ShapeDtypeStruct((ROWS, STEPS, COLS), BF16),
            jax.ShapeDtypeStruct((ROWS, STEPS, COLS), BF16),
            jax.ShapeDtypeStruct((RP, 2 * HD), F32),
        ),
        in_specs=[HBM] * 9,
        out_specs=(SM, HBM, HBM, HBM, HBM),
        scratch_shapes=[
            pltpu.SMEM((ROWS,), jnp.int32),
            pltpu.SMEM((NG * ROWS,), jnp.int32),
            pltpu.SMEM((4, ROWS), jnp.int32),
            pltpu.VMEM((NG * ROWS,), jnp.int32),
            pltpu.VMEM((ROWS, STEPS, 2 * HD), BF16),
            pltpu.VMEM((STEPS, ROWS, 8, 2 * HD), BF16),
            pltpu.VMEM((ROWS, 16, 128), F32),
            pltpu.VMEM((RP, 2 * HD), F32),
            pltpu.VMEM((NG, 16, 128), BF16),
            pltpu.SMEM((NG,), jnp.int32),
            pltpu.VMEM((16, 16, 128), BF16),
            pltpu.VMEM((COLS,), BF16),
            pltpu.VMEM((ROWS, STEPS, COLS), BF16),
            pltpu.VMEM((ROWS, STEPS, COLS), BF16),
            pltpu.VMEM((SLOTS, PAGE, 2 * HD), BF16),
            pltpu.VMEM((2 * HD, D), BF16),
            pltpu.VMEM((ROWS, STEPS, 640), BF16),
            pltpu.VMEM((RP, 640), F32),
            pltpu.VMEM((NG, HALF, 2 * HD), BF16),
            pltpu.VMEM((NG, HALF, 2 * HD), BF16),
            pltpu.VMEM((MOVED, HALF, 2 * HD), BF16),
            pltpu.VMEM((NG, 16, 128), BF16),
            pltpu.VMEM((2 * RP, HD), F32),
            pltpu.VMEM((128, HD), F32),
            pltpu.VMEM((128, HD), F32),
            pltpu.VMEM((RP, HD), F32),
            pltpu.VMEM((4, RP, HD), jnp.int32),
            pltpu.VMEM((SLOTS + 1, 2 * RP, PAGE), F32),
            pltpu.VMEM((NT, BLK, 128), BF16),
            pltpu.VMEM((8, BLK, 128), BF16),
            pltpu.VMEM((48, 128), BF16),
            pltpu.VMEM((32, 128), BF16),
            pltpu.VMEM((6, BLK, 128), BF16),
            pltpu.VMEM((4, BLK, 128), BF16),
            pltpu.VMEM((16, 8, 128), F32),
            pltpu.VMEM((NG, 8, 128), F32),
            pltpu.VMEM((NG, 8, 128), F32),
            pltpu.VMEM((3, RP, 128), F32),
            pltpu.VMEM((1, 128), F32),
            pltpu.VMEM((NT, 1, 128), F32),
            DMA((11,)),
            DMA(()),
            DMA((3,)),
            DMA((3,)),
            DMA(()),
            DMA(()),
            DMA(()),
            DMA(()),
            DMA(()),
            DMA(()),
            DMA((16,)),
            DMA((16,)),
            DMA(()),
            DMA(()),
        ],
        compiler_params=pltpu.CompilerParams(
            collective_id=0, has_side_effects=True, vmem_limit_bytes=58 << 20
        ),
        name="layer",
    )(
        lengths, destination, pb, queries.transpose(1, 0, 2), new_kv, kv, out_weight,
        residual.transpose(1, 0, 2), norm_gain,
    )
    kva, upd, nrm = pl.pallas_call(
        place_kernel,
        out_shape=(
            jax.ShapeDtypeStruct((SLOTS, PAGE, 2 * HD), BF16),
            jax.ShapeDtypeStruct((ROWS, STEPS, COLS), BF16),
            jax.ShapeDtypeStruct((ROWS, STEPS, COLS), BF16),
        ),
        in_specs=[SM, SM, SM, SM, HBM, HBM, VM, HBM, HBM],
        out_specs=(HBM, HBM, HBM),
        scratch_shapes=[
            pltpu.VMEM((SLOTS, PAGE, 2 * HD), BF16),
            DMA((SLOTS,)),
            DMA((3,)),
        ],
        compiler_params=pltpu.CompilerParams(vmem_limit_bytes=60 << 20),
        name="place",
    )(table, lengths, pb, pa, kv, moved, fresh, upd, nrm)
    return kva[None, None], upd.transpose(1, 0, 2), nrm.transpose(1, 0, 2)


def solution(mesh):
    in_specs = (
        P("group"),
        P(),
        P("group", None),
        P("group", None),
        P("group", "tp", None, None, None),
        P(None, "group", "tp"),
        P(None, "group", None, None),
        P(None, "group", None),
        P("tp", None),
        P("tp"),
    )
    out_specs = (P("group", "tp", None, None, None), P(None, "group", "tp"), P(None, "group", "tp"))
    return jax.shard_map(
        on_device, mesh=mesh, in_specs=in_specs, out_specs=out_specs, check_vma=False
    )
```

```python
import jax
import jax.numpy as jnp
from jax import lax
from jax.experimental import pallas as pl
from jax.experimental.pallas import tpu as pltpu
from jax.sharding import PartitionSpec as P

MESH = pl.DeviceIdType.MESH
NG = 32
NT = 16
ROWS = 13
STEPS = 2
SLOTS = 16
PAGE = 128
HD = 128
RP = 32
D = 5120
COLS = D // NT
BLK = 80
F32 = jnp.float32
BF16 = jnp.bfloat16

A_SRC, A_STAY, A_POS = 0, 16, 32
TABLE = 48
MOVED = 11
HALF = PAGE // 2


def torus_offsets():
    found = []
    for ky in range(4):
        for kx in range(4):
            for kc in range(2):
                if (ky, kx, kc) != (0, 0, 0):
                    found.append((min(ky, 4 - ky) + min(kx, 4 - kx), ky, kx, kc))
    return sorted(found, key=lambda o: -o[0])


def layer_kernel(
    lens_in, dest_in, pb_in, q_in, nkv_in, kv, w, res, gain_in,
    table, moved, upd_out, nrm_out, fresh_out,
    length_of, dest, pb, dest_row, q, nkv, build, fresh, pack, slots,
    mine, gain, upd, nrm, kvv, wv, res_win, res32, sbuf, recv, comp, pkt, qs, nks, nvs, lens, pages_of, score,
    part, land1, half1, half2, land2, relay, back, back_out, back_in, hid, sq_own, sq_all,
    load_sem, keep_sem, swap_send, swap_recv, page_send, page_recv, pkt_send, pkt_recv, back_send, back_recv,
    rs_send, rs_recv, sq_send, sq_recv,
):
    g = lax.axis_index("group")
    t = lax.axis_index("tp")
    parity = lax.rem(t, 2)
    get_kv = pltpu.make_async_copy(kv, kvv, load_sem.at[0])
    get_w = pltpu.make_async_copy(w, wv, load_sem.at[1])
    get_res = pltpu.make_async_copy(
        res.at[:, :, pl.ds(pl.multiple_of((t // 2) * 640, 128), 640)], res_win, load_sem.at[2]
    )
    get_gain = pltpu.make_async_copy(gain_in, gain, load_sem.at[3])
    small = [
        pltpu.make_async_copy(src, dst, load_sem.at[4 + n])
        for n, (src, dst) in enumerate(
            (
                (dest_in, dest_row), (dest_in, dest), (lens_in, length_of), (pb_in, pb),
                (nkv_in, nkv), (q_in, q),
            )
        )
    ]
    for load in small:
        load.start()
    get_kv.start()
    get_gain.start()
    get_w.start()
    get_res.start()

    zs = [lax.rem(t + o, NT) for o in range(NT)]

    def at_z(o):
        return zs[o % NT]

    core, x, y = lax.rem(g, 2), lax.rem(g // 2, 4), g // 8
    ys = [lax.rem(y + k, 4) * 8 for k in range(4)]
    xs = [lax.rem(x + k, 4) * 2 for k in range(4)]
    cs = [core, 1 - core]
    ys_to = [ys[k] + core * (ys[-k % 4] - ys[k]) for k in range(4)]
    xs_to = [xs[k] + core * (xs[-k % 4] - xs[k]) for k in range(4)]
    offsets = torus_offsets()
    peers = [ys_to[ky] + xs_to[kx] + cs[kc] for _, ky, kx, kc in offsets]

    barrier = pltpu.get_barrier_semaphore()
    for d in peers:
        pl.semaphore_signal(barrier, inc=1, device_id=(d, t), device_id_type=MESH)
    for o in range(1, NT):
        pl.semaphore_signal(barrier, inc=1, device_id=(g, zs[o]), device_id_type=MESH)

    build[...] = jnp.zeros_like(build)
    for load in small:
        load.wait()
    base = g * ROWS
    dest_all = dest_row[...].reshape(1, NG * ROWS)
    lane = lax.broadcasted_iota(jnp.int32, (16, NG * ROWS), 1)
    row = lax.broadcasted_iota(jnp.int32, (16, NG * ROWS), 0)
    anchor = jnp.max(jnp.where(dest_all == base + row, lane, 0), axis=1, keepdims=True)
    peer_row = lax.broadcasted_iota(jnp.int32, (NG, 1), 0)
    peer_col = jnp.full((NG, 1), -1, jnp.int32)
    for n, d in enumerate(peers):
        peer_col = jnp.where(peer_row == n, d, peer_col)
    lane = lax.broadcasted_iota(jnp.int32, (NG, NG * ROWS), 1)
    taken = (lane >= base) & (lane < base + ROWS)
    taken = taken & (dest_all >= peer_col * ROWS) & (dest_all < peer_col * ROWS + ROWS)
    taker = jnp.max(jnp.where(taken, lane - base, 0), axis=1, keepdims=True)

    rid = lax.broadcasted_iota(jnp.int32, (RP, 208), 0)
    cid = lax.broadcasted_iota(jnp.int32, (RP, 208), 1)
    pick = (cid == ((rid & 1) * ROWS + (rid >> 1)) * 8 + t // 2) & (rid < STEPS * ROWS)
    tokens = jnp.dot(
        pick.astype(F32).astype(BF16),
        nkv[...].astype(F32).reshape(208, 2 * HD).astype(BF16),
        preferred_element_type=F32,
    )
    fresh[...] = tokens
    put_fresh = pltpu.make_async_copy(fresh, fresh_out, load_sem.at[10])
    put_fresh.start()
    lane = lax.broadcasted_iota(jnp.int32, (1, 128), 1)
    homes = jnp.full((1, 128), -2, jnp.int32)
    count = 0
    for r in range(ROWS):
        anc = anchor[r, 0]
        loc = anc - base
        stay = (loc >= 0) & (loc < ROWS)
        home = anc // ROWS
        homes = jnp.where(lane == r, home, homes)
        table[A_SRC + r] = jnp.where(stay, loc, home)
        table[A_STAY + r] = stay.astype(jnp.int32)
        table[A_POS + r] = count
        count = count + jnp.where(stay, 0, 1)
        asked = q[r].astype(F32)
        build[r, 0:2] = asked[:, :HD]
        build[r, 2:4] = asked[:, HD:]
        build[r, 4:6] = tokens[2 * r : 2 * r + 2, :HD]
        build[r, 6:8] = tokens[2 * r : 2 * r + 2, HD:]
        length = length_of[r]
        build[r, 8:9] = jnp.full((1, HD), (length >> 7) * PAGE, jnp.int32).astype(F32)
        build[r, 9:10] = jnp.full((1, HD), length & (PAGE - 1), jnp.int32).astype(F32)
        mine[r] = build[r].astype(BF16)
    giver = jnp.max(jnp.where(peer_col == homes, lane, 0), axis=1, keepdims=True)
    for n in range(NG - 1):
        pack[n] = mine[giver[n, 0]]
        slots[n] = taker[n, 0]
    pl.semaphore_wait(barrier, NG + NT - 2)

    def group_copy(src, dst, send_sem, recv_sem, d):
        return pltpu.make_async_remote_copy(
            src_ref=src, dst_ref=dst, send_sem=send_sem, recv_sem=recv_sem,
            device_id=(d, t), device_id_type=MESH,
        )

    def all_copies(src, dst, send_sem, recv_sem):
        most = pl.ds(0, NG - 1)
        return group_copy(src.at[most], dst.at[most], send_sem, recv_sem, peers[0])

    for n, d in enumerate(peers):
        group_copy(pack.at[n], pkt.at[g], pkt_send, pkt_recv, d).start()
    packets = all_copies(pack, pkt, pkt_send, pkt_recv)
    get_kv.wait()

    half = pl.ds(pl.multiple_of(parity * HALF, HALF), HALF)

    def send_pages(first, last):
        for n in range(first, last):
            d = peers[n]
            sbuf[n] = kvv[pb[0, slots[n]], half, :]
            group_copy(sbuf.at[n], recv.at[g], page_send, page_recv, d).start()

    send_pages(0, 4)

    get_res.wait()
    res32[...] = jnp.zeros_like(res32)
    for a in range(ROWS):
        res32[2 * a : 2 * a + 2, :] = res_win[a].astype(F32)
    qs[...] = jnp.zeros_like(qs)
    nks[...] = jnp.zeros_like(nks)
    nvs[...] = jnp.zeros_like(nvs)
    lens[...] = jnp.zeros_like(lens)
    pages_of[...] = jnp.full_like(pages_of, -1)
    get_gain.wait()
    packets.wait_recv()
    send_pages(4, 8)

    for i in range(ROWS):
        to = dest[base + i]
        loc = to - base
        stay = ((loc >= 0) & (loc < ROWS)).astype(jnp.int32)
        near = mine[loc * stay].astype(F32)
        far = pkt[(to // ROWS) * (1 - stay)].astype(F32)
        got = jnp.where(stay == 1, near, far)
        qs[2 * i : 2 * i + 2, :] = got[0:2]
        qs[RP + 2 * i : RP + 2 * i + 2, :] = got[2:4]
        nks[2 * i : 2 * i + 2, :] = got[4:6]
        nvs[2 * i : 2 * i + 2, :] = got[6:8]
        lens[2 * i : 2 * i + 2, :] = jnp.broadcast_to(got[8:9] + got[9:10], (2, HD))
        need = 1 + stay * (((length_of[loc * stay] + (STEPS + PAGE - 1)) >> 7) - 1)
        for j in range(4):
            page = jnp.where(j < need, pb[j, i], -1)
            pages_of[j, 2 * i : 2 * i + 2, :] = jnp.full((2, HD), page, jnp.int32)

    qa = qs[...].astype(BF16)
    row_all = lax.broadcasted_iota(jnp.int32, (2 * RP, PAGE), 0) & (RP - 1)
    lane = lax.broadcasted_iota(jnp.int32, (2 * RP, PAGE), 1)
    row_b = row_all >> 1
    lane_f = lane.astype(F32)
    row_len = jnp.concatenate([lens[...], lens[...]], axis=0)
    row_page = [jnp.concatenate([pages_of[j], pages_of[j]], axis=0) for j in range(4)]
    sc = lax.dot_general(
        qa, nks[...].astype(BF16), (((1,), (1,)), ((), ())), preferred_element_type=F32
    ) * (HD**-0.5)
    sc = jnp.where(((lane >> 1) == row_b) & ((lane & 1) <= (row_all & 1)), sc, -1e30)
    score[SLOTS] = sc
    top = sc
    for c in range(SLOTS):
        sc = lax.dot_general(
            qa, kvv[c, :, :HD], (((1,), (1,)), ((), ())), preferred_element_type=F32
        ) * (HD**-0.5)
        held = jnp.zeros_like(row_len)
        for j in range(4):
            held = jnp.where(row_page[j] == c, row_len - j * PAGE, held)
        sc = jnp.where(lane_f < held, sc, -1e30)
        score[c] = sc
        top = jnp.maximum(top, sc)
    send_pages(8, 12)
    top = jnp.max(top, axis=1, keepdims=True)
    weight = jnp.exp(score[SLOTS] - top)
    total = weight
    mixed = jnp.dot(weight.astype(BF16), nvs[...].astype(BF16), preferred_element_type=F32)
    for c in range(SLOTS):
        weight = jnp.exp(score[c] - top)
        total = total + weight
        mixed = mixed + jnp.dot(
            weight.astype(BF16), kvv[c, :, HD:], preferred_element_type=F32
        )
    mixed = mixed / jnp.sum(total, axis=1, keepdims=True)
    att = jnp.concatenate([mixed[:RP], mixed[RP:]], axis=1).astype(BF16)

    get_w.wait()
    low = lax.broadcasted_iota(jnp.int32, (16, 128), 1) < 64

    def project(m):
        pair = lax.rem(t // 2 + m, NT // 2)
        columns = pl.ds(pl.multiple_of(pair * 640, 128), 640)
        out = jnp.dot(att, wv[:, columns], preferred_element_type=F32)
        mid = out[:, 256:384]
        left, right = 2 * pair, 2 * pair + 1
        part[left, 0:32] = out[:, 0:128].astype(BF16)
        part[left, 32:64] = out[:, 128:256].astype(BF16)
        part[left, 64:80] = jnp.where(low, mid[:16], pltpu.roll(mid[16:], 64, 1)).astype(BF16)
        part[right, 0:32] = out[:, 384:512].astype(BF16)
        part[right, 32:64] = out[:, 512:640].astype(BF16)
        part[right, 64:80] = jnp.where(low, pltpu.roll(mid[:16], 64, 1), mid[16:]).astype(BF16)

    def z_copy(n, src, dst, o):
        return pltpu.make_async_remote_copy(
            src_ref=src, dst_ref=dst, send_sem=rs_send.at[n], recv_sem=rs_recv.at[n],
            device_id=(g, at_z(o)), device_id_type=MESH,
        )

    first = {
        1: z_copy(1, part.at[at_z(-7)], land1.at[1], -2),
        5: z_copy(5, part.at[at_z(7)], land1.at[5], 2),
        8: z_copy(8, part.at[at_z(8), pl.ds(0, 48)], half1, -3),
        9: z_copy(9, part.at[at_z(8), pl.ds(48, 32)], half2, 3),
        0: z_copy(0, part.at[at_z(-6)], land1.at[0], -1),
        4: z_copy(4, part.at[at_z(6)], land1.at[4], 1),
        3: z_copy(3, part.at[at_z(-4)], land1.at[3], -2),
        7: z_copy(7, part.at[at_z(4)], land1.at[7], 2),
        2: z_copy(2, part.at[at_z(-3)], land1.at[2], -1),
        6: z_copy(6, part.at[at_z(3)], land1.at[6], 1),
        10: z_copy(10, part.at[at_z(-1)], land2.at[0], -1),
        11: z_copy(11, part.at[at_z(1)], land2.at[1], 1),
    }
    for pairs, ready in (((4, 3, 5), (1, 5, 8, 9, 0, 4)), ((2, 6, 1, 7), (3, 7, 2, 6)), ((0,), (10, 11))):
        for m in pairs:
            project(m)
        for n in ready:
            first[n].start()
    send_pages(12, 22)
    second = [
        z_copy(12, relay.at[0], land2.at[2], -5),
        z_copy(13, relay.at[1], land2.at[3], 5),
        z_copy(14, relay.at[2], land2.at[4], -2),
        z_copy(15, relay.at[3], land2.at[5], 2),
    ]
    for n, o, a, b, c in ((0, -5, 0, 1, 8), (1, 5, 4, 5, 9)):
        first[a].wait_recv()
        first[b].wait_recv()
        first[c].wait_recv()
        whole = part[at_z(o)].astype(F32) + land1[a].astype(F32) + land1[b].astype(F32)
        if n == 0:
            relay[n, 0:48] = (whole[0:48] + half1[...].astype(F32)).astype(BF16)
            relay[n, 48:80] = whole[48:80].astype(BF16)
        else:
            relay[n, 0:48] = whole[0:48].astype(BF16)
            relay[n, 48:80] = (whole[48:80] + half2[...].astype(F32)).astype(BF16)
        second[n].start()
    for n, o, a, b in ((2, -2, 2, 3), (3, 2, 6, 7)):
        first[a].wait_recv()
        first[b].wait_recv()
        relay[n] = (
            part[at_z(o)].astype(F32) + land1[a].astype(F32) + land1[b].astype(F32)
        ).astype(BF16)
        second[n].start()
    send_pages(22, 31)
    acc = part[t].astype(F32)
    first[10].wait_recv()
    first[11].wait_recv()
    acc = acc + land2[0].astype(F32) + land2[1].astype(F32)
    for n in (2, 3):
        second[n].wait_recv()
        acc = acc + land2[2 + n].astype(F32)

    pages = all_copies(sbuf, recv, page_send, page_recv)
    pages.wait_recv()
    for j in range(MOVED):
        source = 0
        for r in range(ROWS):
            counts = (1 - table[A_STAY + r]) * (table[A_POS + r] == j).astype(jnp.int32)
            source = source + counts * table[A_SRC + r]
        comp[j] = recv[source]

    def swap_copy(n, first, count):
        some = pl.ds(first, count)
        return pltpu.make_async_remote_copy(
            src_ref=comp.at[some], dst_ref=moved.at[some, half],
            send_sem=swap_send.at[n], recv_sem=swap_recv.at[n],
            device_id=(g, t + 1 - 2 * parity), device_id_type=MESH,
        )

    swaps = [swap_copy(0, 0, 3), swap_copy(1, 3, 4), swap_copy(2, 7, 4)]
    swaps[0].start()
    keep = pltpu.make_async_copy(comp, moved.at[:, half], keep_sem)
    keep.start()
    for n in (0, 1):
        second[n].wait_recv()
        acc = acc + land2[2 + n].astype(F32)

    back[...] = jnp.zeros_like(back)
    tail = jnp.concatenate([acc[64:80], pltpu.roll(acc[64:80], 64, 1)], axis=0)
    for i in range(ROWS):
        back[i, 0:2] = acc[2 * i : 2 * i + 2]
        back[i, 2:4] = acc[32 + 2 * i : 34 + 2 * i]
        back[i, 4:6] = tail[2 * i : 2 * i + 2]

    for n, d in enumerate(peers):
        back_out[n] = back[slots[n]]
        group_copy(back_out.at[n], back_in.at[g], back_send, back_recv, d).start()
    returns = all_copies(back_out, back_in, back_send, back_recv)
    swaps[1].start()

    hid[...] = jnp.zeros_like(hid)
    returns.wait_recv()
    for r in range(ROWS):
        at = table[A_SRC + r]
        stay = table[A_STAY + r]
        row = jnp.where(stay == 1, back[at * stay], back_in[at * (1 - stay)])
        for j in range(3):
            hid[j, 2 * r : 2 * r + 2, :] = row[2 * j : 2 * j + 2]

    even = parity == 0
    mid = res32[:, 256:384]
    sum_a = hid[0] + jnp.where(even, res32[:, 0:128], res32[:, 384:512])
    sum_b = hid[1] + jnp.where(even, res32[:, 128:256], res32[:, 512:640])
    sum_h = hid[2] + jnp.where(even, mid, pltpu.roll(mid, 64, 1))
    own = lax.broadcasted_iota(jnp.int32, (RP, 128), 1) < 64
    sum_h = jnp.where(own, sum_h, 0.0)
    square = jnp.sum(sum_a * sum_a + sum_b * sum_b + sum_h * sum_h, axis=1, keepdims=True)
    diag = lax.broadcasted_iota(jnp.int32, (RP, 128), 0) == lax.broadcasted_iota(
        jnp.int32, (RP, 128), 1
    )
    sq_own[...] = jnp.sum(jnp.where(diag, square, 0.0), axis=0, keepdims=True)

    for o in (8, 7, 9, 6, 10, 5, 11, 4, 12, 3, 13, 2, 14, 1, 15):
        pltpu.make_async_remote_copy(
            src_ref=sq_own, dst_ref=sq_all.at[o], send_sem=sq_send, recv_sem=sq_recv,
            device_id=(g, zs[o]), device_id_type=MESH,
        ).start()
    swaps[2].start()
    most = pl.ds(1, NT - 1)
    squares = pltpu.make_async_remote_copy(
        src_ref=sq_all.at[most], dst_ref=sq_all.at[most], send_sem=sq_send, recv_sem=sq_recv,
        device_id=(g, zs[1]), device_id_type=MESH,
    )
    tail = sum_h[:, 0:64]
    value = jnp.where(
        even,
        jnp.concatenate([sum_a, sum_b, tail], axis=1),
        jnp.concatenate([tail, sum_a, sum_b], axis=1),
    )
    for a in range(ROWS):
        upd[a] = value[2 * a : 2 * a + 2, :].astype(BF16)
    put_upd = pltpu.make_async_copy(upd, upd_out, load_sem.at[0])
    put_upd.start()
    scaled = value * gain[...].astype(F32).reshape(1, COLS)
    whole = sq_own[...]
    squares.wait_recv()
    for k in range(1, NT):
        whole = whole + sq_all[k]
    inverse = lax.rsqrt(whole * (1.0 / D) + 1e-6)
    factor = jnp.sum(jnp.where(diag, inverse, 0.0), axis=1, keepdims=True)
    scaled = scaled * factor
    for a in range(ROWS):
        nrm[a] = scaled[2 * a : 2 * a + 2, :].astype(BF16)
    put_nrm = pltpu.make_async_copy(nrm, nrm_out, load_sem.at[1])
    put_nrm.start()

    for copy in first.values():
        copy.wait_send()
    for copy in second:
        copy.wait_send()
    packets.wait_send()
    returns.wait_send()
    squares.wait_send()
    pages.wait_send()
    keep.wait()
    for copy in swaps:
        copy.wait()
    put_fresh.wait()
    put_upd.wait()
    put_nrm.wait()


def place_kernel(
    table, lens, pb, pa, kv, moved, fresh, upd_in, nrm_in, kva, upd, nrm, buf, page_sem, out_sem
):
    passed = [
        pltpu.make_async_copy(upd_in, upd, out_sem.at[1]),
        pltpu.make_async_copy(nrm_in, nrm, out_sem.at[2]),
    ]
    for copy in passed:
        copy.start()

    def fetch(r, carry):
        need = (lens[r] + (STEPS + PAGE - 1)) >> 7
        at = table[A_SRC + r]
        stay = table[A_STAY + r]

        @pl.when(stay == 0)
        def _():
            c = pa[0, r]
            pltpu.make_async_copy(moved.at[table[A_POS + r]], buf.at[c], page_sem.at[c]).start()

        @pl.when(stay == 1)
        def _():
            def page(j, carry):
                c = pa[j, r]
                pltpu.make_async_copy(kv.at[pb[j, at]], buf.at[c], page_sem.at[c]).start()
                return carry

            lax.fori_loop(0, need, page, 0)

        return carry

    lax.fori_loop(0, ROWS, fetch, 0)
    lane_row = lax.broadcasted_iota(jnp.int32, (16, 2 * HD), 0)
    for c in range(SLOTS):
        pltpu.make_async_copy(kv.at[0], buf.at[c], page_sem.at[c]).wait()

    def patch(r, s, p, both):
        c = pa[p >> 7, r]
        e = p & (PAGE - 1)
        base = pl.multiple_of((e >> 4) << 4, 16)
        block = buf[c, pl.ds(base, 16), :].astype(F32)
        block = jnp.where(lane_row == (e & 15), fresh[pl.ds(2 * r + s, 1), :], block)
        if both:
            block = jnp.where(lane_row == (e & 15) + 1, fresh[pl.ds(2 * r + 1, 1), :], block)
        buf[c, pl.ds(base, 16), :] = block.astype(BF16)

    def write(r, carry):
        p = lens[r]
        patch(r, 0, p, True)

        @pl.when((p & 15) == 15)
        def _():
            patch(r, 1, p + 1, False)

        return carry

    lax.fori_loop(0, ROWS, write, 0)
    out = pltpu.make_async_copy(buf, kva, out_sem.at[0])
    out.start()
    for copy in passed:
        copy.wait()
    out.wait()


VM = pl.BlockSpec(memory_space=pltpu.VMEM)
SM = pl.BlockSpec(memory_space=pltpu.SMEM)
HBM = pl.BlockSpec(memory_space=pltpu.HBM)
DMA = pltpu.SemaphoreType.DMA


def on_device(
    lengths, destination, page_before, page_after, kv_cache,
    queries, new_kv, residual, out_weight, norm_gain,
):
    kv = kv_cache[0, 0]
    pb, pa = page_before.T, page_after.T
    table, moved, upd, nrm, fresh = pl.pallas_call(
        layer_kernel,
        out_shape=(
            jax.ShapeDtypeStruct((TABLE,), jnp.int32),
            jax.ShapeDtypeStruct((MOVED, PAGE, 2 * HD), BF16),
            jax.ShapeDtypeStruct((ROWS, STEPS, COLS), BF16),
            jax.ShapeDtypeStruct((ROWS, STEPS, COLS), BF16),
            jax.ShapeDtypeStruct((RP, 2 * HD), F32),
        ),
        in_specs=[HBM] * 9,
        out_specs=(SM, HBM, HBM, HBM, HBM),
        scratch_shapes=[
            pltpu.SMEM((ROWS,), jnp.int32),
            pltpu.SMEM((NG * ROWS,), jnp.int32),
            pltpu.SMEM((4, ROWS), jnp.int32),
            pltpu.VMEM((NG * ROWS,), jnp.int32),
            pltpu.VMEM((ROWS, STEPS, 2 * HD), BF16),
            pltpu.VMEM((STEPS, ROWS, 8, 2 * HD), BF16),
            pltpu.VMEM((ROWS, 16, 128), F32),
            pltpu.VMEM((RP, 2 * HD), F32),
            pltpu.VMEM((NG, 16, 128), BF16),
            pltpu.SMEM((NG,), jnp.int32),
            pltpu.VMEM((16, 16, 128), BF16),
            pltpu.VMEM((COLS,), BF16),
            pltpu.VMEM((ROWS, STEPS, COLS), BF16),
            pltpu.VMEM((ROWS, STEPS, COLS), BF16),
            pltpu.VMEM((SLOTS, PAGE, 2 * HD), BF16),
            pltpu.VMEM((2 * HD, D), BF16),
            pltpu.VMEM((ROWS, STEPS, 640), BF16),
            pltpu.VMEM((RP, 640), F32),
            pltpu.VMEM((NG, HALF, 2 * HD), BF16),
            pltpu.VMEM((NG, HALF, 2 * HD), BF16),
            pltpu.VMEM((MOVED, HALF, 2 * HD), BF16),
            pltpu.VMEM((NG, 16, 128), BF16),
            pltpu.VMEM((2 * RP, HD), F32),
            pltpu.VMEM((128, HD), F32),
            pltpu.VMEM((128, HD), F32),
            pltpu.VMEM((RP, HD), F32),
            pltpu.VMEM((4, RP, HD), jnp.int32),
            pltpu.VMEM((SLOTS + 1, 2 * RP, PAGE), F32),
            pltpu.VMEM((NT, BLK, 128), BF16),
            pltpu.VMEM((8, BLK, 128), BF16),
            pltpu.VMEM((48, 128), BF16),
            pltpu.VMEM((32, 128), BF16),
            pltpu.VMEM((6, BLK, 128), BF16),
            pltpu.VMEM((4, BLK, 128), BF16),
            pltpu.VMEM((16, 8, 128), F32),
            pltpu.VMEM((NG, 8, 128), F32),
            pltpu.VMEM((NG, 8, 128), F32),
            pltpu.VMEM((3, RP, 128), F32),
            pltpu.VMEM((1, 128), F32),
            pltpu.VMEM((NT, 1, 128), F32),
            DMA((11,)),
            DMA(()),
            DMA((3,)),
            DMA((3,)),
            DMA(()),
            DMA(()),
            DMA(()),
            DMA(()),
            DMA(()),
            DMA(()),
            DMA((16,)),
            DMA((16,)),
            DMA(()),
            DMA(()),
        ],
        compiler_params=pltpu.CompilerParams(
            collective_id=0, has_side_effects=True, vmem_limit_bytes=58 << 20
        ),
        name="layer",
    )(
        lengths, destination, pb, queries.transpose(1, 0, 2), new_kv, kv, out_weight,
        residual.transpose(1, 0, 2), norm_gain,
    )
    kva, upd, nrm = pl.pallas_call(
        place_kernel,
        out_shape=(
            jax.ShapeDtypeStruct((SLOTS, PAGE, 2 * HD), BF16),
            jax.ShapeDtypeStruct((ROWS, STEPS, COLS), BF16),
            jax.ShapeDtypeStruct((ROWS, STEPS, COLS), BF16),
        ),
        in_specs=[SM, SM, SM, SM, HBM, HBM, VM, HBM, HBM],
        out_specs=(HBM, HBM, HBM),
        scratch_shapes=[
            pltpu.VMEM((SLOTS, PAGE, 2 * HD), BF16),
            DMA((SLOTS,)),
            DMA((3,)),
        ],
        compiler_params=pltpu.CompilerParams(vmem_limit_bytes=60 << 20),
        name="place",
    )(table, lengths, pb, pa, kv, moved, fresh, upd, nrm)
    return kva[None, None], upd.transpose(1, 0, 2), nrm.transpose(1, 0, 2)


def solution(mesh):
    in_specs = (
        P("group"),
        P(),
        P("group", None),
        P("group", None),
        P("group", "tp", None, None, None),
        P(None, "group", "tp"),
        P(None, "group", None, None),
        P(None, "group", None),
        P("tp", None),
        P("tp"),
    )
    out_specs = (P("group", "tp", None, None, None), P(None, "group", "tp"), P(None, "group", "tp"))
    return jax.shard_map(
        on_device, mesh=mesh, in_specs=in_specs, out_specs=out_specs, check_vma=False
    )
```
